512 devices in a mesh: wide: 128 (over z, y, core), narrow: 4 (over x).
Axes of the slice: x: 4, y: 8, z: 8, core: 2. Of those that a mesh axis runs over, the one named last changes fastest.
Arguments:
- statistics: float32 [128, 2, 512, 512], P(None, None, 'wide', 'narrow'), as said below
- gradients: bfloat16 [128, 512, 512], P(None, 'wide', 'narrow'), may hold values from -6 to 6
- assign: int32 [128, 2], replicated, may hold values from 0 to 127, as said below
- counts: int32 [128], replicated, may hold values from 0 to 2, as said below
Outputs:
- inverse_roots: float32 [128, 2, 512, 512], P(None, None, 'wide', 'narrow')
- root_diagonals: float32 [128, 2, 512], P(None, None, 'wide')
- directions: bfloat16 [128, 2, 512, 512], P('wide')
The draws below stay inside these ranges and needn't reach their ends.
Inputs may be any that keep to these rules, and one draw needn't show every extreme that they name: `assign`: for worker w the first counts[w] entries are the blocks it roots; over all workers these name every block of 0 to 127 exactly once. Entries at slots from counts[w] on are arbitrary block numbers. The counts sum to 128; some worker roots 2 blocks and some none. `statistics`: every factor is symmetric and positive definite.
All inputs are finite; a program needn't handle non-finite values.
Results may differ from the reference program's by a relative error of at most 0.0065.
Values may be sent and summed in bfloat16 or wider, within the bound.
A program may use at most 64 MiB of HBM per device.

```python
import math
import jax
import jax.numpy as jnp
from jax import lax

BLOCK = 512
ITERS = 2
WORKERS = 128
SLOTS = 2
BLOCKS = 128


def routing(key):
    subkeys = jax.random.split(key, 5)
    pair_count = WORKERS // 2
    worker_loads = jax.random.randint(subkeys[0], (pair_count,), 0, SLOTS + 1)
    forced_pair = jax.random.randint(subkeys[1], (), 0, pair_count)
    worker_loads = jnp.where(jnp.arange(pair_count) == forced_pair, SLOTS, worker_loads)
    paired = jnp.concatenate([worker_loads, SLOTS - worker_loads])
    shuffle = jax.random.permutation(subkeys[2], WORKERS)
    counts = paired[shuffle]
    block_order = jax.random.permutation(subkeys[3], BLOCKS)
    offsets = jnp.cumsum(counts) - counts
    slot_index = jnp.arange(SLOTS)
    positions = jnp.clip(offsets[:, None] + slot_index[None, :], 0, BLOCKS - 1)
    occupied = slot_index[None, :] < counts[:, None]
    filler = jax.random.randint(subkeys[4], (WORKERS, SLOTS), 0, BLOCKS)
    assign = jnp.where(occupied, block_order[positions], filler)
    return (assign.astype(jnp.int32), counts.astype(jnp.int32))


def draw_assign(key, part):
    assign, counts = routing(key)
    return assign


def draw_counts(key, part):
    assign, counts = routing(key)
    return counts


def draw_statistics(key, part):
    key = jax.random.fold_in(key, 11)
    subkeys = jax.random.split(key, 2)
    factor_shape = (BLOCKS * 2, BLOCK, BLOCK)
    log_top = math.log(10.0)
    samples = jax.random.normal(subkeys[0], factor_shape)
    products = jnp.einsum('kir,kjr->kij', samples, samples, precision=lax.Precision.HIGHEST) / BLOCK
    products = 0.5 * (products + jnp.swapaxes(products, 1, 2))
    identity = jnp.eye(BLOCK, dtype=jnp.float32)
    central = products + 0.05 * identity
    scales = jnp.exp(jax.random.uniform(subkeys[1], (BLOCKS * 2, BLOCK), minval=0.0, maxval=log_top))
    result = 0.002 * central * scales[:, :, None] * scales[:, None, :]
    return result.reshape(BLOCKS, 2, BLOCK, BLOCK).astype(jnp.float32)


def level_of(own_key, dims, cuts, least, high):
    def one(position, shards_of):
        steps = jax.random.uniform(jax.random.fold_in(jax.random.fold_in(own_key, 6), position), (shards_of,), jnp.float32, least / len(cuts), high / len(cuts))
        return jnp.repeat(jnp.exp(steps), dims[position] // shards_of).reshape((-1,) + (1,) * (len(dims) - position - 1))

    level = one(*cuts[0])
    for cut in cuts[1:]:
        level = level * one(*cut)
    return level


def noise(key, dims, scale, reach, cuts=(), kind=jnp.bfloat16):
    values = jax.random.normal(key, dims, jnp.float32) * scale
    if len(cuts) > 0:
        values = level_of(key, dims, cuts, -0.22, 0.18) * values
    return jnp.clip(values, min=-reach, max=reach).astype(kind)


def setup_inputs(seed: int = 0) -> dict:
    key_of = jax.random.split(jax.random.key(seed), 5)
    return {
        "statistics": draw_statistics(jax.random.fold_in(key_of[4], 71), 0),
        "gradients": noise(key_of[1], (BLOCKS, BLOCK, BLOCK), 1.0, 6.0, ((1, 128), (2, 4))),
        "assign": draw_assign(jax.random.fold_in(key_of[4], 71), 0),
        "counts": draw_counts(jax.random.fold_in(key_of[4], 71), 0),
    }


def batched_product(first, second):
    return jnp.einsum('kij,kjl->kil', first, second, precision=lax.Precision.HIGHEST, preferred_element_type=jnp.float32)

def inverse_fourth_root(factors):
    identity = jnp.eye(factors.shape[-1], dtype=jnp.float32)
    frobenius = jnp.sqrt(lax.optimization_barrier(jnp.sum(factors * factors, axis=(1, 2), keepdims=True)))
    scaling = 2.5 / frobenius
    current = scaling * factors
    iterate = current
    for iteration in range(ITERS):
        step_matrix = 0.25 * (5.0 * identity - current)
        if iteration == 0:
            iterate = jnp.sqrt(jnp.sqrt(scaling)) * step_matrix
        else:
            iterate = batched_product(iterate, step_matrix)
        if iteration + 1 < ITERS:
            square = batched_product(step_matrix, step_matrix)
            current = batched_product(batched_product(square, square), current)
    return iterate

def precondition(root_pair, gradient):
    left_root = root_pair[0].astype(jnp.bfloat16)
    right_root = root_pair[1].astype(jnp.bfloat16)
    half_product = jnp.dot(left_root, gradient, preferred_element_type=jnp.float32).astype(jnp.bfloat16)
    return jnp.dot(half_product, right_root, preferred_element_type=jnp.float32).astype(jnp.bfloat16)

def reference(statistics, gradients, assign, counts):
    full_roots = lax.map(inverse_fourth_root, statistics)
    on_diagonal = jnp.eye(BLOCK, dtype=bool)
    root_diagonals = jnp.diagonal(full_roots, axis1=2, axis2=3)
    inverse_roots = jnp.where(on_diagonal, jnp.zeros_like(full_roots), full_roots)
    listed = assign.reshape(WORKERS * SLOTS).astype(jnp.int32)
    occupied = (jnp.arange(SLOTS, dtype=jnp.int32)[None, :] < counts[:, None]).reshape(WORKERS * SLOTS)

    def one_slot(operands):
        block_index, keep = operands
        direction = precondition(full_roots[block_index], gradients[block_index])
        return jnp.where(keep, direction, jnp.zeros_like(direction))
    directions = lax.map(one_slot, (listed, occupied)).reshape(WORKERS, SLOTS, BLOCK, BLOCK)
    return (inverse_roots, root_diagonals, directions)
```

```python
import jax
import jax.numpy as jnp
from jax import lax
from jax.experimental import pallas as pl
from jax.experimental.pallas import tpu as pltpu
from jax.sharding import PartitionSpec as P

BLOCK = 512
CHIPS = 64
NARROW = 4
MESH = pl.DeviceIdType.MESH
F32 = jnp.float32
BF16 = jnp.bfloat16


def dot(first, second):
    return jnp.dot(first, second, preferred_element_type=F32)


def dot_nt(first, second):
    return lax.dot_general(
        first, second, (((1,), (1,)), ((), ())), preferred_element_type=F32
    )


def iota(shape, axis):
    return lax.broadcasted_iota(jnp.int32, shape, axis)


def send(src, dst, send_sem, recv_sem, wide, narrow):
    pltpu.make_async_remote_copy(
        src_ref=src,
        dst_ref=dst,
        send_sem=send_sem,
        recv_sem=recv_sem,
        device_id=(wide, narrow),
        device_id_type=MESH,
    ).start()


def wait(ref, sem):
    pltpu.make_async_copy(ref, ref, sem).wait()


def kernel(
    stat_ref,
    grad_ref,
    assign_ref,
    counts_ref,
    counts_smem,
    roots_ref,
    diag_ref,
    dirs_ref,
    out1,
    in1,
    flat1,
    out2,
    in2,
    gflat,
    gout1,
    gin1,
    gflat1,
    gout2,
    gin2,
    grad_half,
    factor,
    work,
    low_a,
    low_b,
    low_root,
    half_out,
    half_in,
    dir_out,
    out3,
    in3,
    flat3,
    out4,
    in4,
    select_t,
    send1,
    recv1,
    send2,
    recv2,
    gsend1,
    grecv1,
    gsend2,
    grecv2,
    half_send,
    half_recv,
    prod_send,
    prod_recv,
    dir_send,
    dir_recv,
    send3,
    recv3,
    send4,
    recv4,
):
    wide = lax.axis_index("wide")
    me_n = lax.axis_index("narrow")
    me_j = wide // 2
    me_c = wide % 2
    me_y = me_j % 8
    me_z = me_j // 8
    me_g = me_n * 2 + me_c

    def group_mate(i):
        g = lax.rem(me_g + i, 8)
        return g, me_j * 2 + g % 2, g // 2

    def far_mate(i):
        y = lax.rem(me_y + i % 8, 8)
        z = lax.rem(me_z + i // 8, 8)
        return z * 8 + y

    barrier = pltpu.get_barrier_semaphore()

    @pl.loop(1, 64)
    def _(i):
        pl.semaphore_signal(
            barrier, inc=1, device_id=(far_mate(i) * 2 + me_c, me_n), device_id_type=MESH
        )

    @pl.loop(1, 8)
    def _(i):
        _, w, n = group_mate(i)
        pl.semaphore_signal(barrier, inc=1, device_id=(w, n), device_id_type=MESH)

    block_of_row = iota((128, 128), 0)
    one_hots = []
    picks = []
    for slot in range(2):
        listed = assign_ref[slot : slot + 1, :]
        hot = block_of_row == listed
        one_hots.append(jnp.where(hot, 1.0, 0.0).astype(BF16))
        kept = jnp.logical_and(hot, counts_ref[...] > slot)
        picks.append(jnp.where(kept, 1.0, 0.0).astype(BF16))
    gathers = []
    for m in range(4):
        par, slot = m // 2, m % 2
        spread = jnp.where(
            iota((CHIPS, 128), 1) == 2 * iota((CHIPS, 128), 0) + par, 1.0, 0.0
        ).astype(BF16)
        gathers.append(dot_nt(spread, one_hots[slot]).astype(BF16))
        spread_t = jnp.where(
            iota((128, 128), 0) == 2 * iota((128, 128), 1) + par, 1.0, 0.0
        ).astype(BF16)
        select_t[:, 128 * m : 128 * m + 128] = dot(picks[slot], spread_t).astype(BF16)
    gather = jnp.concatenate(gathers, axis=0)

    for k in range(2):
        for r in range(4):
            x = stat_ref[pl.ds(k * 4 + r, 128, stride=8), :]
            high = x.astype(BF16)
            rest = (x - high.astype(F32)).astype(BF16)
            upper = iota((128, 128), 1) + 128 * me_n >= 4 * wide + r
            mixed = jnp.where(upper, high.astype(F32), rest.astype(F32)).astype(BF16)
            picked = dot(gather, mixed).astype(BF16)
            for m in range(4):
                out1[m * 2 + k, r * 64 : r * 64 + 64, :] = picked[m * 64 : m * 64 + 64]
    gflat[...] = grad_ref[...].astype(F32)
    for r in range(4):
        x = gflat[pl.ds(r, 128, stride=4), :].astype(BF16)
        picked = dot(gather, x).astype(BF16)
        for m in range(4):
            gout1[m, r * 64 : r * 64 + 64, :] = picked[m * 64 : m * 64 + 64]
    in1[me_g] = out1[me_g]

    pl.semaphore_wait(barrier, 70)

    @pl.loop(1, 8)
    def _(i):
        g, w, n = group_mate(i)
        send(out1.at[g], in1.at[me_g], send1, recv1, w, n)

    g_core = me_n // 2
    g_place = (me_n % 2) * 2 + me_c
    for d in range(1, 4):
        m = lax.rem(me_n + d, 4)
        send(gout1.at[m], gin1.at[g_place], gsend1, grecv1, me_j * 2 + g_core, m)

    @pl.when(g_core != me_c)
    def _():
        send(gout1.at[me_n], gin1.at[g_place], gsend1, grecv1, me_j * 2 + g_core, me_n)

    @pl.when(g_core == me_c)
    def _():
        gin1[g_place] = gout1[me_n]

    wait(in1.at[pl.ds(0, 7)], recv1)
    for g in range(8):
        flat1[g * 256 : g * 256 + 256, :] = in1[g].astype(F32)

    @pl.loop(0, CHIPS, unroll=8)
    def _(i):
        out2[i] = flat1[pl.ds(i, 32, stride=64), :].astype(BF16)

    in2[me_j] = out2[me_j]

    @pl.loop(1, CHIPS)
    def _(i):
        j = far_mate(i)
        send(out2.at[j], in2.at[me_j], send2, recv2, j * 2 + me_c, me_n)

    @pl.when(g_core == me_c)
    def _():
        wait(gin1.at[pl.ds(0, 3)], grecv1)

    @pl.when(g_core != me_c)
    def _():
        wait(gin1, grecv1)

    for g in range(4):
        gflat1[g * 256 : g * 256 + 256, :] = gin1[g].astype(F32)

    @pl.loop(0, CHIPS, unroll=8)
    def _(i):
        gout2[i] = gflat1[pl.ds(i, 16, stride=64), :].astype(BF16)

    gin2[me_j] = gout2[me_j]

    @pl.loop(1, CHIPS)
    def _(i):
        j = far_mate(i)
        send(gout2.at[j], gin2.at[me_j], gsend2, grecv2, j * 2 + me_c, me_n)

    wait(in2.at[pl.ds(0, CHIPS - 1)], recv2)

    @pl.loop(0, CHIPS, unroll=4)
    def _(i):
        x = in2[i].astype(F32)
        rows = pl.ds(pl.multiple_of(i * 8, 8), 8)
        for n in range(4):
            factor[rows, 128 * n : 128 * n + 128] = x[8 * n : 8 * n + 8]

    eye = iota((BLOCK, BLOCK), 0) == iota((BLOCK, BLOCK), 1)
    received = factor[...]
    a = received + jnp.where(eye, 0.0, received.T)
    total = jnp.sum(jnp.sum(a * a, axis=0, keepdims=True), axis=1, keepdims=True)
    scaling = 2.5 / jnp.sqrt(total)
    c = scaling * a
    factor[...] = c
    low_a[...] = c.astype(BF16)
    e = dot(low_a[...], low_a[...]) - 10.0 * factor[...]
    work[...] = e
    low_b[...] = e.astype(BF16)
    f = 50.0 * work[...] + dot(low_b[...], low_b[...])
    low_b[...] = f.astype(BF16)
    c2 = (625.0 / 256.0) * factor[...] + (1.0 / 256.0) * dot(low_b[...], low_a[...])
    work[...] = c2
    low_b[...] = c2.astype(BF16)
    scale4 = jnp.sqrt(jnp.sqrt(scaling)) * (1.0 / 16.0)
    tail = dot(low_a[...], low_b[...]) - 5.0 * (factor[...] + work[...])
    root = scale4 * (jnp.where(eye, 25.0, 0.0) + tail)
    work[...] = root
    low_root[...] = root.astype(BF16)

    @pl.loop(0, CHIPS, unroll=4)
    def _(i):
        rows = pl.ds(pl.multiple_of(i * 8, 8), 8)
        parts = [work[rows, 128 * n : 128 * n + 128] for n in range(4)]
        out3[i] = jnp.concatenate(parts, axis=0).astype(BF16)

    in3[me_j] = out3[me_j]

    @pl.loop(1, CHIPS)
    def _(i):
        j = far_mate(i)
        send(out3.at[j], in3.at[me_j], send3, recv3, j * 2 + me_c, me_n)

    wait(gin2.at[pl.ds(0, CHIPS - 1)], grecv2)

    @pl.loop(0, CHIPS // 2, unroll=4)
    def _(i):
        x0 = gin2[2 * i].astype(F32)
        x1 = gin2[2 * i + 1].astype(F32)
        rows = pl.ds(pl.multiple_of(i * 16, 16), 16)
        for n in range(2):
            both = jnp.concatenate([x0[8 * n : 8 * n + 8], x1[8 * n : 8 * n + 8]], axis=0)
            grad_half[me_c, rows, 128 * n : 128 * n + 128] = both.astype(BF16)

    @pl.when(me_c == 1)
    def _():
        send(grad_half.at[1], grad_half.at[1], half_send, half_recv, me_j * 2, me_n)
        wait(half_in, prod_recv)
        product = dot(half_in[...], low_root[...])
        taken = counts_smem[2 * me_j + me_n // 2] > me_n % 2
        product = product * jnp.where(taken, 1.0, 0.0)
        dir_out[...] = product.astype(BF16)
        for d in range(1, 4):
            n = lax.rem(me_n + d, 4)
            send(
                dir_out,
                dirs_ref.at[me_n % 2],
                dir_send,
                dir_recv.at[me_n % 2],
                me_j * 2 + me_n // 2,
                n,
            )

    @pl.when(me_c == 0)
    def _():
        wait(grad_half.at[1], half_recv)
        for k in range(2):
            half_out[:, 256 * k : 256 * k + 256] = dot(low_root[...], grad_half[k]).astype(BF16)
        send(half_out, half_in, prod_send, prod_recv, me_j * 2 + 1, me_n)

    @pl.when(jnp.logical_and(me_c == 1, me_n // 2 == 0))
    def _():
        send(
            dir_out,
            dirs_ref.at[me_n % 2],
            dir_send,
            dir_recv.at[me_n % 2],
            me_j * 2,
            me_n,
        )

    @pl.when(jnp.logical_and(me_c == 1, me_n // 2 == 1))
    def _():
        dirs_ref[me_n % 2] = dir_out[...]

    wait(in3.at[pl.ds(0, CHIPS - 1)], recv3)

    @pl.loop(0, CHIPS, unroll=8)
    def _(i):
        flat3[pl.ds(pl.multiple_of(i * 32, 32), 32), :] = in3[i].astype(F32)

    for q in range(32):
        n, c_, r = q // 8, (q // 4) % 2, q % 4
        out4[n * 2 + c_, r * 64 : r * 64 + 64, :] = flat3[pl.ds(q, 64, stride=32), :].astype(BF16)
    for c_ in range(2):
        diag = jnp.zeros((16, 64), F32)
        for r in range(4):
            rows = flat3[pl.ds((me_j // 16) * 8 + c_ * 4 + r, 64, stride=32), :].astype(BF16)
            place = jnp.logical_and(
                iota((16, 128), 0) == r, iota((16, 128), 1) == (8 * me_j + 4 * c_ + r) % 128
            )
            diag = diag + dot_nt(jnp.where(place, 1.0, 0.0).astype(BF16), rows)
        padded = jnp.concatenate([diag, jnp.zeros((16, 64), F32)], axis=1).astype(BF16)
        for n in range(4):
            out4[n * 2 + c_, 256:272, :] = padded
    in4[me_g] = out4[me_g]

    @pl.loop(1, 8)
    def _(i):
        g, w, n = group_mate(i)
        send(out4.at[g], in4.at[me_g], send4, recv4, w, n)

    wait(in4.at[pl.ds(0, 7)], recv4)
    for k in range(2):
        for r in range(4):
            acc = jnp.zeros((128, 128), F32)
            for m in range(4):
                acc = acc + dot(
                    select_t[:, 128 * m : 128 * m + 64], in4[m * 2 + k, r * 64 : r * 64 + 64, :]
                )
            on_diag = iota((128, 128), 1) + 128 * me_n == 4 * wide + r
            roots_ref[pl.ds(k * 4 + r, 128, stride=8), :] = jnp.where(on_diag, 0.0, acc)
        dg = jnp.zeros((128, 16), F32)
        for m in range(4):
            dg = dg + dot_nt(select_t[:, 128 * m : 128 * m + 128], in4[m * 2 + k, 256:272, :])
        diag_ref[k] = dg

    @pl.when(jnp.logical_and(me_c == 1, me_n == 2))
    def _():
        wait(dirs_ref.at[1], dir_recv.at[1])

    @pl.when(jnp.logical_and(me_c == 1, me_n == 3))
    def _():
        wait(dirs_ref.at[0], dir_recv.at[0])

    @pl.when(jnp.logical_or(me_c == 0, me_n < 2))
    def _():
        wait(dirs_ref.at[0], dir_recv.at[0])
        wait(dirs_ref.at[1], dir_recv.at[1])

    wait(in1.at[pl.ds(0, 7)], send1)
    wait(in2.at[pl.ds(0, CHIPS - 1)], send2)
    wait(gin2.at[pl.ds(0, CHIPS - 1)], gsend2)
    wait(in3.at[pl.ds(0, CHIPS - 1)], send3)
    wait(in4.at[pl.ds(0, 7)], send4)

    @pl.when(g_core == me_c)
    def _():
        wait(gin1.at[pl.ds(0, 3)], gsend1)

    @pl.when(g_core != me_c)
    def _():
        wait(gin1, gsend1)

    @pl.when(me_c == 0)
    def _():
        wait(half_in, prod_send)

    @pl.when(me_c == 1)
    def _():
        wait(grad_half.at[1], half_send)

    @pl.when(jnp.logical_and(me_c == 1, me_n // 2 == 0))
    def _():
        wait(dirs_ref, dir_send)
        wait(dirs_ref, dir_send)

    @pl.when(jnp.logical_and(me_c == 1, me_n // 2 == 1))
    def _():
        wait(dirs_ref, dir_send)
        wait(dirs_ref.at[0], dir_send)


def per_device(statistics, gradients, assign, counts):
    blocks = statistics.shape[0]
    vmem = pl.BlockSpec(memory_space=pltpu.VMEM)
    smem = pl.BlockSpec(memory_space=pltpu.SMEM)
    square = (BLOCK, BLOCK)
    scratch = [
        pltpu.VMEM((8, 256, 128), BF16),
        pltpu.VMEM((8, 256, 128), BF16),
        pltpu.VMEM((2048, 128), F32),
        pltpu.VMEM((64, 32, 128), BF16),
        pltpu.VMEM((64, 32, 128), BF16),
        pltpu.VMEM((512, 128), F32),
        pltpu.VMEM((4, 256, 128), BF16),
        pltpu.VMEM((4, 256, 128), BF16),
        pltpu.VMEM((1024, 128), F32),
        pltpu.VMEM((64, 16, 128), BF16),
        pltpu.VMEM((64, 16, 128), BF16),
        pltpu.VMEM((2, BLOCK, 256), BF16),
        pltpu.VMEM(square, F32),
        pltpu.VMEM(square, F32),
        pltpu.VMEM(square, BF16),
        pltpu.VMEM(square, BF16),
        pltpu.VMEM(square, BF16),
        pltpu.VMEM(square, BF16),
        pltpu.VMEM(square, BF16),
        pltpu.VMEM(square, BF16),
        pltpu.VMEM((64, 32, 128), BF16),
        pltpu.VMEM((64, 32, 128), BF16),
        pltpu.VMEM((2048, 128), F32),
        pltpu.VMEM((8, 272, 128), BF16),
        pltpu.VMEM((8, 272, 128), BF16),
        pltpu.VMEM((128, 512), BF16),
    ]
    dma = pltpu.SemaphoreType.DMA
    scratch += [dma] * 12 + [dma, dma((2,))] + [dma] * 4
    roots, diags, dirs = pl.pallas_call(
        kernel,
        out_shape=[
            jax.ShapeDtypeStruct((blocks * 8, 128), F32),
            jax.ShapeDtypeStruct((2, blocks, 16), F32),
            jax.ShapeDtypeStruct((2, BLOCK, BLOCK), BF16),
        ],
        in_specs=[vmem, vmem, vmem, vmem, smem],
        out_specs=[vmem, vmem, vmem],
        scratch_shapes=scratch,
        compiler_params=pltpu.CompilerParams(
            collective_id=0, has_side_effects=True, vmem_limit_bytes=48 * 2**20
        ),
        cost_estimate=pl.CostEstimate(
            flops=2 * 6 * BLOCK**3, bytes_accessed=4 * 2**20, transcendentals=0
        ),
        name="shampoo_roots",
    )(
        statistics.reshape(blocks * 8, 128),
        gradients.reshape(blocks * 4, 128),
        assign.T,
        counts.reshape(1, -1),
        counts,
    )
    inverse_roots = roots.reshape(statistics.shape)
    root_diagonals = jnp.swapaxes(diags[:, :, :4], 0, 1)
    return inverse_roots, root_diagonals, dirs[None]


def solution(mesh):
    return jax.shard_map(
        per_device,
        mesh=mesh,
        in_specs=(P(None, None, "wide", "narrow"), P(None, "wide", "narrow"), P(), P()),
        out_specs=(
            P(None, None, "wide", "narrow"),
            P(None, None, "wide"),
            P("wide", None, None, None),
        ),
        check_vma=False,
    )
```

```python
import jax
import jax.numpy as jnp
from jax import lax
from jax.experimental import pallas as pl
from jax.experimental.pallas import tpu as pltpu
from jax.sharding import PartitionSpec as P

BLOCK = 512
CHIPS = 64
MESH = pl.DeviceIdType.MESH
F32 = jnp.float32
BF16 = jnp.bfloat16

OWN = 48


def steps(place):
    return place % 8, (place // 8 + 2) % 8


def distance(place):
    return sum(min(s, 8 - s) for s in steps(place))


FAR = sorted(range(32), key=lambda p: -distance(p))
NEAR = sorted((p for p in range(32, 64) if p != OWN), key=lambda p: -distance(p))


def dot(first, second):
    return jnp.dot(first, second, preferred_element_type=F32)


def dot_nt(first, second):
    return lax.dot_general(
        first, second, (((1,), (1,)), ((), ())), preferred_element_type=F32
    )


def iota(shape, axis):
    return lax.broadcasted_iota(jnp.int32, shape, axis)


def hot(condition):
    return jnp.where(condition, 1.0, 0.0).astype(BF16)


def send(src, dst, send_sem, recv_sem, wide, narrow):
    pltpu.make_async_remote_copy(
        src_ref=src,
        dst_ref=dst,
        send_sem=send_sem,
        recv_sem=recv_sem,
        device_id=(wide, narrow),
        device_id_type=MESH,
    ).start()


def wait(ref, sem):
    pltpu.make_async_copy(ref, ref, sem).wait()


def kernel(
    stat_hbm,
    grad_hbm,
    assign_hbm,
    counts_hbm,
    roots_ref,
    diag_ref,
    dirs_ref,
    stat_ref,
    grad_ref,
    assign_ref,
    counts_ref,
    out1,
    in1,
    flat1,
    out2,
    in2,
    gflat,
    gspread,
    gout1,
    gin1,
    gmid,
    gout2,
    gin2,
    grows,
    grad,
    factor,
    work,
    low_a,
    low_b,
    low_root,
    half_out,
    half_in,
    dir_out,
    out3,
    in3,
    flat3,
    out4a,
    in4a,
    out4b,
    in4b,
    partial,
    load_sem,
    send1,
    recv1,
    send2,
    recv2,
    gsend1,
    grecv1,
    gsend2,
    grecv2,
    prod_send,
    prod_recv,
    dir_send,
    dir_recv,
    send3,
    recv3,
    send4,
    recv4,
):
    loads = [
        pltpu.make_async_copy(src, dst, load_sem.at[i])
        for i, (src, dst) in enumerate(
            [
                (assign_hbm, assign_ref),
                (counts_hbm, counts_ref),
                (stat_hbm, stat_ref),
                (grad_hbm, grad_ref),
            ]
        )
    ]
    for load in loads:
        load.start()
    wide = lax.axis_index("wide")
    me_n = lax.axis_index("narrow")
    me_j = wide // 2
    me_c = wide % 2
    me_y = me_j % 8
    me_z = me_j // 8
    me_g = me_n * 2 + me_c
    along_y = [(me_y + s) % 8 for s in range(8)]
    along_z = [(me_z + s) % 8 * 8 for s in range(8)]

    def chip(place):
        y, z = steps(place)
        return along_z[z] + along_y[y]

    def group_mate(i):
        g = (me_g + i) % 8
        return g, me_j * 2 + g % 2, g // 2

    barrier = pltpu.get_barrier_semaphore()
    for i in range(1, 8):
        _, w, n = group_mate(i)
        pl.semaphore_signal(barrier, inc=1, device_id=(w, n), device_id_type=MESH)
    for place in FAR + NEAR:
        pl.semaphore_signal(
            barrier, inc=1, device_id=(chip(place) * 2 + me_c, me_n), device_id_type=MESH
        )

    def chips_at(shape, axis, sign):
        place = iota(shape, axis)
        y, z = place % 8, (place // 8 + 2) % 8
        return (me_z + sign * z + 8) % 8 * 8 + (me_y + sign * y + 8) % 8

    loads[0].wait()
    loads[1].wait()
    to_worker = 2 * chips_at((CHIPS, 128), 0, 1)
    from_worker = 2 * chips_at((128, CHIPS), 1, -1)
    listed = []
    taken = []
    for slot in range(2):
        match = iota((128, 128), 0) == assign_ref[slot : slot + 1, :]
        listed.append(hot(match))
        taken.append(hot(jnp.logical_and(match, counts_ref[...] > slot)))
    gathers = []
    selects = []
    for m in range(4):
        par, slot = m // 2, m % 2
        pick = hot(iota((CHIPS, 128), 1) == to_worker + par)
        gathers.append(dot_nt(pick, listed[slot]).astype(BF16))
        place = hot(iota((128, CHIPS), 0) == from_worker + par)
        selects.append(dot(taken[slot], place).astype(BF16))
    gather = jnp.concatenate(gathers, axis=0)

    loads[2].wait()
    for k in range(2):
        for r in range(4):
            x = stat_ref[pl.ds(k * 4 + r, 128, stride=8), :]
            high = x.astype(BF16).astype(F32)
            upper = iota((128, 128), 1) + 128 * me_n >= 4 * wide + r
            mixed = jnp.where(upper, high, x - high).astype(BF16)
            picked = dot(gather, mixed).astype(BF16)
            for m in range(4):
                for half in range(2):
                    start = m * 64 + half * 32
                    out1[half, m * 2 + k, r * 32 : r * 32 + 32, :] = picked[start : start + 32]
    for half in range(2):
        in1[half, me_g] = out1[half, me_g]
    loads[3].wait()
    gflat[...] = grad_ref[...].astype(F32)
    for r in range(4):
        x = gflat[pl.ds(r, 128, stride=4), :].astype(BF16)
        picked = dot(gather, x)
        for m in range(4):
            gspread[pl.ds(m * 4 + r, 64, stride=16), :] = picked[m * 64 : m * 64 + 64]
    gout1[...] = gspread[...].reshape(CHIPS, 16, 128).astype(BF16)
    gin1[me_j] = gout1[OWN]

    pl.semaphore_wait(barrier, 70)

    for half in range(2):
        for i in (4, 5, 3, 2, 6, 7, 1):
            g, w, n = group_mate(i)
            send(
                out1.at[half, g], in1.at[half, me_g], send1.at[half], recv1.at[half], w, n
            )
    for place in FAR + NEAR:
        send(
            gout1.at[place], gin1.at[me_j], gsend1, grecv1, chip(place) * 2 + me_c, me_n
        )

    for half, places in enumerate((FAR, NEAR)):
        wait(in1.at[half, pl.ds(0, 7)], recv1.at[half])
        flat1[half] = in1[half].reshape(1024, 128).astype(F32)
        if half == 1:
            out2[OWN] = flat1[1, pl.ds(OWN - 32, 32, stride=32), :].astype(BF16)
            in2[me_j] = out2[OWN]
        for place in places:
            out2[place] = flat1[half, pl.ds(place % 32, 32, stride=32), :].astype(BF16)
            send(
                out2.at[place], in2.at[me_j], send2, recv2, chip(place) * 2 + me_c, me_n
            )

    wait(gin1.at[pl.ds(0, CHIPS - 1)], grecv1)
    gmid[...] = gin1[...].reshape(1024, 128).astype(F32)
    for m in range(4):
        for r in range(4):
            gout2[m, r * 64 : r * 64 + 64, :] = gmid[pl.ds(m * 4 + r, 64, stride=16), :].astype(
                BF16
            )
    for d in (2, 1, 3):
        m = (me_n + d) % 4
        send(gout2.at[m], gin2.at[me_g], gsend2, grecv2, me_j * 2, m)

    @pl.when(me_c == 1)
    def _():
        send(gout2.at[me_n], gin2.at[me_g], gsend2, grecv2, me_j * 2, me_n)

    @pl.when(me_c == 0)
    def _():
        gin2[me_g] = gout2[me_n]

    wait(in2.at[pl.ds(0, CHIPS - 1)], recv2)
    for j in range(CHIPS):
        x = in2[j].astype(F32)
        for n in range(4):
            factor[8 * j : 8 * j + 8, 128 * n : 128 * n + 128] = x[8 * n : 8 * n + 8]

    eye = iota((BLOCK, BLOCK), 0) == iota((BLOCK, BLOCK), 1)
    received = factor[...]
    a = received + jnp.where(eye, 0.0, received.T)
    total = jnp.sum(jnp.sum(a * a, axis=0, keepdims=True), axis=1, keepdims=True)
    scaling = 2.5 / jnp.sqrt(total)
    c = scaling * a
    factor[...] = c
    low_a[...] = c.astype(BF16)
    e = dot(low_a[...], low_a[...]) - 10.0 * factor[...]
    work[...] = e
    low_b[...] = e.astype(BF16)
    f = 50.0 * work[...] + dot(low_b[...], low_b[...])
    low_b[...] = f.astype(BF16)
    c2 = (625.0 / 256.0) * factor[...] + (1.0 / 256.0) * dot(low_b[...], low_a[...])
    work[...] = c2
    low_b[...] = c2.astype(BF16)
    scale4 = jnp.sqrt(jnp.sqrt(scaling)) * (1.0 / 16.0)
    tail = dot(low_a[...], low_b[...]) - 5.0 * (factor[...] + work[...])
    root = scale4 * (jnp.where(eye, 25.0, 0.0) + tail)
    work[...] = root
    low_root[...] = root.astype(BF16)

    def rows_for(place):
        rows = pl.ds(pl.multiple_of(chip(place) * 8, 8), 8)
        parts = [work[rows, 128 * n : 128 * n + 128] for n in range(4)]
        return jnp.concatenate(parts, axis=0).astype(BF16)

    for half, places in enumerate((FAR, NEAR)):
        for place in places:
            out3[place] = rows_for(place)
            send(
                out3.at[place],
                in3.at[place],
                send3.at[half],
                recv3.at[half],
                chip(place) * 2 + me_c,
                me_n,
            )
    in3[OWN] = rows_for(OWN)

    @pl.when(me_c == 0)
    def _():
        wait(gin2.at[pl.ds(0, 7)], grecv2)
        for g in range(8):
            for r in range(4):
                grows[g // 2, pl.ds(g % 2 * 4 + r, 64, stride=8), :] = gin2[
                    g, r * 64 : r * 64 + 64, :
                ].astype(F32)
        for n in range(4):
            grad[:, 128 * n : 128 * n + 128] = grows[n].astype(BF16)
        half_out[...] = dot(low_root[...], grad[...]).astype(BF16)
        send(half_out, half_in, prod_send, prod_recv, me_j * 2 + 1, me_n)

    @pl.when(me_c == 1)
    def _():
        mine = jnp.logical_and(
            iota((1, 128), 1) == 2 * me_j + me_n // 2, counts_ref[...] > me_n % 2
        )
        keep = jnp.sum(jnp.where(mine, 1.0, 0.0), axis=1, keepdims=True)
        wait(half_in, prod_recv)
        dir_out[...] = (dot(half_in[...], low_root[...]) * keep).astype(BF16)
        for d in (2, 1, 3):
            send(
                dir_out,
                dirs_ref.at[me_n % 2],
                dir_send,
                dir_recv.at[me_n % 2],
                me_j * 2 + me_n // 2,
                (me_n + d) % 4,
            )

    @pl.when(jnp.logical_and(me_c == 1, me_n // 2 == 0))
    def _():
        send(
            dir_out,
            dirs_ref.at[me_n % 2],
            dir_send,
            dir_recv.at[me_n % 2],
            me_j * 2,
            me_n,
        )

    @pl.when(jnp.logical_and(me_c == 1, me_n // 2 == 1))
    def _():
        dirs_ref[me_n % 2] = dir_out[...]

    wait(in3.at[pl.ds(0, 32)], recv3.at[0])
    flat3[:1024] = in3[:32].reshape(1024, 128).astype(F32)
    for q in range(32):
        out4a[q // 4, q % 4 * 32 : q % 4 * 32 + 32, :] = flat3[pl.ds(q, 32, stride=32), :].astype(
            BF16
        )
    in4a[me_g] = out4a[me_g]
    for i in (4, 5, 3, 2, 6, 7, 1):
        g, w, n = group_mate(i)
        send(out4a.at[g], in4a.at[me_g], send4.at[0], recv4.at[0], w, n)

    wait(in3.at[pl.ds(0, 31)], recv3.at[1])
    flat3[1024:] = in3[32:].reshape(1024, 128).astype(F32)
    for q in range(32):
        out4b[q // 4, q % 4 * 32 : q % 4 * 32 + 32, :] = flat3[
            pl.ds(1024 + q, 32, stride=32), :
        ].astype(BF16)
    for core in range(2):
        diag = jnp.zeros((16, CHIPS), F32)
        for r in range(4):
            rows = flat3[pl.ds((me_j // 16) * 8 + core * 4 + r, CHIPS, stride=32), :].astype(BF16)
            place = jnp.logical_and(
                iota((16, 128), 0) == r, iota((16, 128), 1) == (8 * me_j + 4 * core + r) % 128
            )
            diag = diag + dot_nt(hot(place), rows)
        padded = jnp.concatenate([diag, jnp.zeros((16, CHIPS), F32)], axis=1).astype(BF16)
        for n in range(4):
            out4b[n * 2 + core, 128:144, :] = padded
    in4b[me_g] = out4b[me_g]
    for i in (4, 5, 3, 2, 6, 7, 1):
        g, w, n = group_mate(i)
        send(out4b.at[g], in4b.at[me_g], send4.at[1], recv4.at[1], w, n)

    def picked_rows(received, k, r, half):
        select = jnp.concatenate([s[:, half * 32 : half * 32 + 32] for s in selects], axis=1)
        rows = [received[m * 2 + k, r * 32 : r * 32 + 32, :] for m in range(4)]
        return dot(select, jnp.concatenate(rows, axis=0))

    wait(in4a.at[pl.ds(0, 7)], recv4.at[0])
    for k in range(2):
        for r in range(4):
            partial[k * 4 + r] = picked_rows(in4a, k, r, 0)
    wait(in4b.at[pl.ds(0, 7)], recv4.at[1])
    for k in range(2):
        for r in range(4):
            full = partial[k * 4 + r] + picked_rows(in4b, k, r, 1)
            on_diag = iota((128, 128), 1) + 128 * me_n == 4 * wide + r
            roots_ref[pl.ds(k * 4 + r, 128, stride=8), :] = jnp.where(on_diag, 0.0, full)
        diag = jnp.zeros((16, 128), F32)
        for m in range(4):
            diag = diag + dot_nt(in4b[m * 2 + k, 128:144, :][:, :CHIPS], selects[m])
        diag_ref[k] = diag[:4]

    @pl.when(jnp.logical_and(me_c == 1, me_n == 2))
    def _():
        wait(dirs_ref.at[1], dir_recv.at[1])

    @pl.when(jnp.logical_and(me_c == 1, me_n == 3))
    def _():
        wait(dirs_ref.at[0], dir_recv.at[0])

    @pl.when(jnp.logical_or(me_c == 0, me_n < 2))
    def _():
        wait(dirs_ref.at[0], dir_recv.at[0])
        wait(dirs_ref.at[1], dir_recv.at[1])

    for half in range(2):
        wait(in1.at[half, pl.ds(0, 7)], send1.at[half])
    wait(in2.at[pl.ds(0, CHIPS - 1)], send2)
    wait(gin1.at[pl.ds(0, CHIPS - 1)], gsend1)
    wait(in3.at[pl.ds(0, 32)], send3.at[0])
    wait(in3.at[pl.ds(0, 31)], send3.at[1])
    wait(in4a.at[pl.ds(0, 7)], send4.at[0])
    wait(in4b.at[pl.ds(0, 7)], send4.at[1])

    @pl.when(me_c == 0)
    def _():
        wait(gin2.at[pl.ds(0, 3)], gsend2)
        wait(half_in, prod_send)

    @pl.when(me_c == 1)
    def _():
        wait(gin2.at[pl.ds(0, 4)], gsend2)

    @pl.when(jnp.logical_and(me_c == 1, me_n // 2 == 0))
    def _():
        wait(dirs_ref, dir_send)
        wait(dirs_ref, dir_send)

    @pl.when(jnp.logical_and(me_c == 1, me_n // 2 == 1))
    def _():
        wait(dirs_ref, dir_send)
        wait(dirs_ref.at[0], dir_send)


def per_device(statistics, gradients, assign, counts):
    blocks = statistics.shape[0]
    vmem = pl.BlockSpec(memory_space=pltpu.VMEM)
    hbm = pl.BlockSpec(memory_space=pltpu.HBM)
    square = (BLOCK, BLOCK)
    shapes = [
        ((blocks * 8, 128), F32),
        ((blocks * 4, 128), BF16),
        ((2, 128), jnp.int32),
        ((1, 128), jnp.int32),
        ((2, 8, 128, 128), BF16),
        ((2, 8, 128, 128), BF16),
        ((2, 1024, 128), F32),
        ((64, 32, 128), BF16),
        ((64, 32, 128), BF16),
        ((512, 128), F32),
        ((1024, 128), F32),
        ((64, 16, 128), BF16),
        ((64, 16, 128), BF16),
        ((1024, 128), F32),
        ((4, 256, 128), BF16),
        ((8, 256, 128), BF16),
        ((4, 512, 128), F32),
        (square, BF16),
        (square, F32),
        (square, F32),
        (square, BF16),
        (square, BF16),
        (square, BF16),
        (square, BF16),
        (square, BF16),
        (square, BF16),
        ((64, 32, 128), BF16),
        ((64, 32, 128), BF16),
        ((2048, 128), F32),
        ((8, 128, 128), BF16),
        ((8, 128, 128), BF16),
        ((8, 144, 128), BF16),
        ((8, 144, 128), BF16),
        ((8, 128, 128), F32),
    ]
    dma = pltpu.SemaphoreType.DMA
    two = dma((2,))
    scratch = [pltpu.VMEM(shape, dtype) for shape, dtype in shapes]
    scratch += [dma((4,)), two, two] + [dma] * 9 + [two] * 5
    roots, diags, dirs = pl.pallas_call(
        kernel,
        out_shape=[
            jax.ShapeDtypeStruct((blocks * 8, 128), F32),
            jax.ShapeDtypeStruct((2, 4, blocks), F32),
            jax.ShapeDtypeStruct((2, BLOCK, BLOCK), BF16),
        ],
        in_specs=[hbm] * 4,
        out_specs=[vmem, vmem, vmem],
        scratch_shapes=scratch,
        compiler_params=pltpu.CompilerParams(
            collective_id=0, has_side_effects=True, vmem_limit_bytes=40 * 2**20
        ),
        cost_estimate=pl.CostEstimate(
            flops=2 * 6 * BLOCK**3, bytes_accessed=4 * 2**20, transcendentals=0
        ),
        name="shampoo_roots",
    )(
        statistics.reshape(blocks * 8, 128),
        gradients.reshape(blocks * 4, 128),
        assign.T,
        counts.reshape(1, -1),
    )
    inverse_roots = roots.reshape(statistics.shape)
    root_diagonals = jnp.transpose(diags, (2, 0, 1))
    return inverse_roots, root_diagonals, dirs[None]


def solution(mesh):
    return jax.shard_map(
        per_device,
        mesh=mesh,
        in_specs=(P(None, None, "wide", "narrow"), P(None, "wide", "narrow"), P(), P()),
        out_specs=(
            P(None, None, "wide", "narrow"),
            P(None, None, "wide"),
            P("wide", None, None, None),
        ),
        check_vma=False,
    )
```

```python
import jax
import jax.numpy as jnp
from jax import lax
from jax.experimental import pallas as pl
from jax.experimental.pallas import tpu as pltpu
from jax.sharding import PartitionSpec as P

BLOCK = 512
CHIPS = 64
MESH = pl.DeviceIdType.MESH
F32 = jnp.float32
BF16 = jnp.bfloat16


def far_first():
    sizes = [(a, b) for a in range(5) for b in range(5)]
    sizes.sort(key=lambda s: (-(s[0] + s[1]), abs(s[0] - s[1])))
    order = []
    for a, b in sizes:
        for step in ((a, b), (-a, -b), (a, -b), (-a, b)):
            step = (step[0] % 8, step[1] % 8)
            if step not in order:
                order.append(step)
    return order


STEPS = far_first()
OWN = CHIPS - 1
HALVES = (range(32), range(32, OWN))


def dot(first, second):
    return jnp.dot(first, second, preferred_element_type=F32)


def dot_nt(first, second):
    return lax.dot_general(
        first, second, (((1,), (1,)), ((), ())), preferred_element_type=F32
    )


def iota(shape, axis):
    return lax.broadcasted_iota(jnp.int32, shape, axis)


def hot(condition):
    return jnp.where(condition, 1.0, 0.0).astype(BF16)


def send(src, dst, send_sem, recv_sem, wide, narrow):
    pltpu.make_async_remote_copy(
        src_ref=src,
        dst_ref=dst,
        send_sem=send_sem,
        recv_sem=recv_sem,
        device_id=(wide, narrow),
        device_id_type=MESH,
    ).start()


def wait(ref, sem):
    pltpu.make_async_copy(ref, ref, sem).wait()


def kernel(
    stat_hbm,
    grad_hbm,
    assign_hbm,
    counts_hbm,
    roots_ref,
    diag_ref,
    dirs_ref,
    stat_ref,
    grad_ref,
    assign_ref,
    counts_ref,
    out1,
    in1,
    flat1,
    out2,
    in2,
    gflat,
    gspread,
    gout1,
    gin1,
    gmid,
    gout2,
    gin2,
    grows,
    grad,
    factor,
    work,
    low_a,
    low_b,
    low_root,
    half_out,
    half_in,
    dir_out,
    spread3,
    out3,
    in3,
    flat3,
    out4,
    in4,
    flat4,
    partial,
    diag_rows,
    diag_far,
    diag_out,
    diag_in,
    load_sem,
    send1,
    recv1,
    send2,
    recv2,
    gsend1,
    grecv1,
    gsend2,
    grecv2,
    prod_send,
    prod_recv,
    dir_send,
    dir_recv,
    send3,
    recv3,
    send4,
    recv4,
    far_send,
    far_recv,
    diag_send,
    diag_recv,
):
    loads = [
        pltpu.make_async_copy(src, dst, load_sem.at[i])
        for i, (src, dst) in enumerate(
            [
                (assign_hbm, assign_ref),
                (counts_hbm, counts_ref),
                (stat_hbm, stat_ref),
                (grad_hbm, grad_ref),
            ]
        )
    ]
    for load in loads:
        load.start()
    wide = lax.axis_index("wide")
    me_n = lax.axis_index("narrow")
    me_j = wide // 2
    me_c = wide % 2
    me_y = me_j % 8
    me_z = me_j // 8
    me_g = me_n * 2 + me_c
    along_y = [(me_y + s) % 8 for s in range(8)]
    along_z = [(me_z + s) % 8 * 8 for s in range(8)]

    def chip(place):
        y, z = STEPS[place]
        return along_z[z] + along_y[y]

    def group_mate(i):
        g = (me_g + i) % 8
        return g, me_j * 2 + g % 2, g // 2

    barrier = pltpu.get_barrier_semaphore()
    for i in range(1, 8):
        _, w, n = group_mate(i)
        pl.semaphore_signal(barrier, inc=1, device_id=(w, n), device_id_type=MESH)
    for place in range(OWN):
        pl.semaphore_signal(
            barrier, inc=1, device_id=(chip(place) * 2 + me_c, me_n), device_id_type=MESH
        )

    def steps_column(which):
        tiles = []
        for start in range(0, CHIPS, 8):
            tile = jnp.full((8, 128), STEPS[start][which], jnp.int32)
            for i in range(1, 8):
                tile = jnp.where(iota((8, 128), 0) == i, STEPS[start + i][which], tile)
            tiles.append(tile)
        return jnp.concatenate(tiles, axis=0)

    step_y, step_z = steps_column(0), steps_column(1)
    to_worker = 2 * ((me_z + step_z) % 8 * 8 + (me_y + step_y) % 8)
    from_worker = 2 * ((me_z - step_z + 8) % 8 * 8 + (me_y - step_y + 8) % 8)
    worker = iota((CHIPS, 128), 1)
    loads[0].wait()
    loads[1].wait()
    listed = []
    taken = []
    for slot in range(2):
        match = iota((128, 128), 0) == assign_ref[slot : slot + 1, :]
        listed.append(hot(match))
        taken.append(hot(jnp.logical_and(match, counts_ref[...] > slot)))
    gathers = []
    selects = []
    for m in range(4):
        par, slot = m // 2, m % 2
        gathers.append(dot_nt(hot(worker == to_worker + par), listed[slot]).astype(BF16))
        selects.append(dot_nt(taken[slot], hot(worker == from_worker + par)).astype(BF16))
    gather = jnp.concatenate(gathers, axis=0)

    loads[2].wait()
    for k in range(2):
        for r in range(4):
            x = stat_ref[pl.ds(k * 4 + r, 128, stride=8), :]
            high = x.astype(BF16).astype(F32)
            upper = iota((128, 128), 1) + 128 * me_n >= 4 * wide + r
            mixed = jnp.where(upper, high, x - high).astype(BF16)
            picked = dot(gather, mixed).astype(BF16)
            for m in range(4):
                for half in range(2):
                    start = m * 64 + half * 32
                    out1[half, m * 2 + k, r * 32 : r * 32 + 32, :] = picked[start : start + 32]
    for half in range(2):
        in1[half, me_g] = out1[half, me_g]
    loads[3].wait()
    gflat[...] = grad_ref[...].astype(F32)
    for r in range(4):
        x = gflat[pl.ds(r, 128, stride=4), :].astype(BF16)
        picked = dot(gather, x)
        for m in range(4):
            gspread[pl.ds(m * 4 + r, 64, stride=16), :] = picked[m * 64 : m * 64 + 64]
    gout1[...] = gspread[...].reshape(CHIPS, 16, 128).astype(BF16)
    gin1[me_j] = gout1[OWN]

    pl.semaphore_wait(barrier, 70)

    for half in range(2):
        for i in (4, 5, 3, 2, 6, 7, 1):
            g, w, n = group_mate(i)
            send(
                out1.at[half, g], in1.at[half, me_g], send1.at[half], recv1.at[half], w, n
            )
    for place in range(OWN):
        send(
            gout1.at[place], gin1.at[me_j], gsend1, grecv1, chip(place) * 2 + me_c, me_n
        )

    for half, places in enumerate(HALVES):
        wait(in1.at[half, pl.ds(0, 7)], recv1.at[half])
        flat1[half] = in1[half].reshape(1024, 128).astype(F32)
        if half == 1:
            out2[OWN] = flat1[1, pl.ds(OWN - 32, 32, stride=32), :].astype(BF16)
            in2[me_j] = out2[OWN]
        for place in places:
            out2[place] = flat1[half, pl.ds(place % 32, 32, stride=32), :].astype(BF16)
            send(
                out2.at[place], in2.at[me_j], send2, recv2, chip(place) * 2 + me_c, me_n
            )

    wait(gin1.at[pl.ds(0, CHIPS - 1)], grecv1)
    gmid[...] = gin1[...].reshape(1024, 128).astype(F32)
    for m in range(4):
        for r in range(4):
            gout2[m, r * 64 : r * 64 + 64, :] = gmid[pl.ds(m * 4 + r, 64, stride=16), :].astype(
                BF16
            )
    for d in (2, 1, 3):
        m = (me_n + d) % 4
        send(gout2.at[m], gin2.at[me_g], gsend2, grecv2, me_j * 2, m)

    @pl.when(me_c == 1)
    def _():
        send(gout2.at[me_n], gin2.at[me_g], gsend2, grecv2, me_j * 2, me_n)

    @pl.when(me_c == 0)
    def _():
        gin2[me_g] = gout2[me_n]

    wait(in2.at[pl.ds(0, CHIPS - 1)], recv2)
    for j in range(CHIPS):
        x = in2[j].astype(F32)
        for n in range(4):
            factor[8 * j : 8 * j + 8, 128 * n : 128 * n + 128] = x[8 * n : 8 * n + 8]

    eye = iota((BLOCK, BLOCK), 0) == iota((BLOCK, BLOCK), 1)
    received = factor[...]
    a = received + jnp.where(eye, 0.0, received.T)
    total = jnp.sum(jnp.sum(a * a, axis=0, keepdims=True), axis=1, keepdims=True)
    scaling = 2.5 / jnp.sqrt(total)
    c = scaling * a
    factor[...] = c
    low_a[...] = c.astype(BF16)
    e = dot(low_a[...], low_a[...]) - 10.0 * factor[...]
    work[...] = e
    low_b[...] = e.astype(BF16)
    f = 50.0 * work[...] + dot(low_b[...], low_b[...])
    low_b[...] = f.astype(BF16)
    c2 = (625.0 / 256.0) * factor[...] + (1.0 / 256.0) * dot(low_b[...], low_a[...])
    work[...] = c2
    low_b[...] = c2.astype(BF16)
    scale4 = jnp.sqrt(jnp.sqrt(scaling)) * (1.0 / 16.0)
    tail = dot(low_a[...], low_b[...]) - 5.0 * (factor[...] + work[...])
    root = scale4 * (jnp.where(eye, 25.0, 0.0) + tail)
    work[...] = root
    low_root[...] = root.astype(BF16)
    diagonal = jnp.sum(jnp.where(eye, root, 0.0), axis=0, keepdims=True)
    for n in range(4):
        diag_rows[n] = diagonal[:, 128 * n : 128 * n + 128]

    for half, places in enumerate((range(32), range(32, CHIPS))):
        for i, place in enumerate(places):
            rows = pl.ds(pl.multiple_of(chip(place) * 8, 8), 8)
            for n in range(4):
                spread3[n, i * 8 : i * 8 + 8, :] = work[rows, 128 * n : 128 * n + 128]
        for q in range(32):
            n, core, r = q // 8, q // 4 % 2, q % 4
            out3[half, n * 2 + core, r * 32 : r * 32 + 32, :] = spread3[
                n, pl.ds(core * 4 + r, 32, stride=8), :
            ].astype(BF16)
        in3[half, me_g] = out3[half, me_g]
        for i in (4, 5, 3, 2, 6, 7, 1):
            g, w, n = group_mate(i)
            send(
                out3.at[half, g], in3.at[half, me_g], send3.at[half], recv3.at[half], w, n
            )

    for place in range(OWN):
        send(
            diag_rows.at[chip(place) // 16],
            diag_far.at[place],
            far_send,
            far_recv,
            chip(place) * 2 + me_c,
            me_n,
        )
    diag_far[OWN] = diag_rows[me_j // 16]

    @pl.when(me_c == 0)
    def _():
        wait(gin2.at[pl.ds(0, 7)], grecv2)
        for g in range(8):
            for r in range(4):
                grows[g // 2, pl.ds(g % 2 * 4 + r, 64, stride=8), :] = gin2[
                    g, r * 64 : r * 64 + 64, :
                ].astype(F32)
        for n in range(4):
            grad[:, 128 * n : 128 * n + 128] = grows[n].astype(BF16)
        half_out[...] = dot(low_root[...], grad[...]).astype(BF16)
        send(half_out, half_in, prod_send, prod_recv, me_j * 2 + 1, me_n)

    @pl.when(me_c == 1)
    def _():
        mine = jnp.logical_and(
            iota((1, 128), 1) == 2 * me_j + me_n // 2, counts_ref[...] > me_n % 2
        )
        keep = jnp.sum(jnp.where(mine, 1.0, 0.0), axis=1, keepdims=True)
        wait(half_in, prod_recv)
        dir_out[...] = (dot(half_in[...], low_root[...]) * keep).astype(BF16)
        for d in (2, 1, 3):
            send(
                dir_out,
                dirs_ref.at[me_n % 2],
                dir_send,
                dir_recv.at[me_n % 2],
                me_j * 2 + me_n // 2,
                (me_n + d) % 4,
            )

    @pl.when(jnp.logical_and(me_c == 1, me_n // 2 == 0))
    def _():
        send(
            dir_out,
            dirs_ref.at[me_n % 2],
            dir_send,
            dir_recv.at[me_n % 2],
            me_j * 2,
            me_n,
        )

    @pl.when(jnp.logical_and(me_c == 1, me_n // 2 == 1))
    def _():
        dirs_ref[me_n % 2] = dir_out[...]

    for half, places in enumerate(HALVES):
        wait(in3.at[half, pl.ds(0, 7)], recv3.at[half])
        flat3[half] = in3[half].reshape(1024, 128).astype(F32)
        for place in places:
            out4[place] = flat3[half, pl.ds(place % 32, 32, stride=32), :].astype(BF16)
            send(
                out4.at[place],
                in4.at[place],
                send4,
                recv4.at[half],
                chip(place) * 2 + me_c,
                me_n,
            )
        if half == 1:
            in4[OWN] = flat3[half, pl.ds(OWN % 32, 32, stride=32), :].astype(BF16)

    wait(diag_far.at[pl.ds(0, OWN)], far_recv)
    mine = jnp.logical_and(
        iota((16, 128), 0) < 8, iota((16, 128), 1) == 8 * (me_j % 16) + iota((16, 128), 0)
    )
    far = diag_far[...].reshape(CHIPS, 128).astype(BF16)
    diag_out[...] = jnp.concatenate(
        [dot_nt(hot(mine), far), jnp.zeros((16, CHIPS), F32)], axis=1
    ).astype(BF16)
    diag_in[me_g] = diag_out[...]
    for i in (4, 5, 3, 2, 6, 7, 1):
        g, w, n = group_mate(i)
        send(diag_out, diag_in.at[me_g], diag_send, diag_recv, w, n)

    def picked_rows(k, r, half):
        select = jnp.concatenate([s[:, half * 32 : half * 32 + 32] for s in selects], axis=1)
        starts = [half * 1024 + (m * 2 + k) * 4 + r for m in range(4)]
        rows = [flat4[pl.ds(start, 32, stride=32), :].astype(BF16) for start in starts]
        return dot(select, jnp.concatenate(rows, axis=0))

    wait(in4.at[pl.ds(0, 32)], recv4.at[0])
    flat4[:1024] = in4[:32].reshape(1024, 128).astype(F32)
    for k in range(2):
        for r in range(4):
            partial[k * 4 + r] = picked_rows(k, r, 0)
    wait(diag_in.at[pl.ds(0, 7)], diag_recv)
    for k in range(2):
        diag = jnp.zeros((16, 128), F32)
        for m in range(4):
            diag = diag + dot_nt(diag_in[m * 2 + k][:, :CHIPS], selects[m])
        diag_ref[k] = jnp.where(me_c == 0, diag[0:4], diag[4:8])
    wait(in4.at[pl.ds(0, 31)], recv4.at[1])
    flat4[1024:] = in4[32:].reshape(1024, 128).astype(F32)
    for k in range(2):
        for r in range(4):
            full = partial[k * 4 + r] + picked_rows(k, r, 1)
            on_diag = iota((128, 128), 1) + 128 * me_n == 4 * wide + r
            roots_ref[pl.ds(k * 4 + r, 128, stride=8), :] = jnp.where(on_diag, 0.0, full)

    @pl.when(jnp.logical_and(me_c == 1, me_n == 2))
    def _():
        wait(dirs_ref.at[1], dir_recv.at[1])

    @pl.when(jnp.logical_and(me_c == 1, me_n == 3))
    def _():
        wait(dirs_ref.at[0], dir_recv.at[0])

    @pl.when(jnp.logical_or(me_c == 0, me_n < 2))
    def _():
        wait(dirs_ref.at[0], dir_recv.at[0])
        wait(dirs_ref.at[1], dir_recv.at[1])

    for half in range(2):
        wait(in1.at[half, pl.ds(0, 7)], send1.at[half])
    wait(in2.at[pl.ds(0, CHIPS - 1)], send2)
    wait(gin1.at[pl.ds(0, CHIPS - 1)], gsend1)
    for half in range(2):
        wait(in3.at[half, pl.ds(0, 7)], send3.at[half])
    wait(in4.at[pl.ds(0, CHIPS - 1)], send4)
    wait(diag_far.at[pl.ds(0, OWN)], far_send)
    wait(diag_in.at[pl.ds(0, 7)], diag_send)

    @pl.when(me_c == 0)
    def _():
        wait(gin2.at[pl.ds(0, 3)], gsend2)
        wait(half_in, prod_send)

    @pl.when(me_c == 1)
    def _():
        wait(gin2.at[pl.ds(0, 4)], gsend2)

    @pl.when(jnp.logical_and(me_c == 1, me_n // 2 == 0))
    def _():
        wait(dirs_ref, dir_send)
        wait(dirs_ref, dir_send)

    @pl.when(jnp.logical_and(me_c == 1, me_n // 2 == 1))
    def _():
        wait(dirs_ref, dir_send)
        wait(dirs_ref.at[0], dir_send)


def per_device(statistics, gradients, assign, counts):
    blocks = statistics.shape[0]
    vmem = pl.BlockSpec(memory_space=pltpu.VMEM)
    hbm = pl.BlockSpec(memory_space=pltpu.HBM)
    square = (BLOCK, BLOCK)
    shapes = [
        ((blocks * 8, 128), F32),
        ((blocks * 4, 128), BF16),
        ((2, 128), jnp.int32),
        ((1, 128), jnp.int32),
        ((2, 8, 128, 128), BF16),
        ((2, 8, 128, 128), BF16),
        ((2, 1024, 128), F32),
        ((64, 32, 128), BF16),
        ((64, 32, 128), BF16),
        ((512, 128), F32),
        ((1024, 128), F32),
        ((64, 16, 128), BF16),
        ((64, 16, 128), BF16),
        ((1024, 128), F32),
        ((4, 256, 128), BF16),
        ((8, 256, 128), BF16),
        ((4, 512, 128), F32),
        (square, BF16),
        (square, F32),
        (square, F32),
        (square, BF16),
        (square, BF16),
        (square, BF16),
        (square, BF16),
        (square, BF16),
        (square, BF16),
        ((4, 256, 128), F32),
        ((2, 8, 128, 128), BF16),
        ((2, 8, 128, 128), BF16),
        ((2, 1024, 128), F32),
        ((64, 32, 128), BF16),
        ((64, 32, 128), BF16),
        ((2048, 128), F32),
        ((8, 128, 128), F32),
        ((4, 1, 128), F32),
        ((64, 1, 128), F32),
        ((16, 128), BF16),
        ((8, 16, 128), BF16),
    ]
    dma = pltpu.SemaphoreType.DMA
    two = dma((2,))
    scratch = [pltpu.VMEM(shape, dtype) for shape, dtype in shapes]
    scratch += [dma((4,)), two, two] + [dma] * 9 + [two] * 3 + [dma, two] + [dma] * 4
    roots, diags, dirs = pl.pallas_call(
        kernel,
        out_shape=[
            jax.ShapeDtypeStruct((blocks * 8, 128), F32),
            jax.ShapeDtypeStruct((2, 4, blocks), F32),
            jax.ShapeDtypeStruct((2, BLOCK, BLOCK), BF16),
        ],
        in_specs=[hbm] * 4,
        out_specs=[vmem, vmem, vmem],
        scratch_shapes=scratch,
        compiler_params=pltpu.CompilerParams(
            collective_id=0, has_side_effects=True, vmem_limit_bytes=40 * 2**20
        ),
        cost_estimate=pl.CostEstimate(
            flops=2 * 6 * BLOCK**3, bytes_accessed=4 * 2**20, transcendentals=0
        ),
        name="shampoo_roots",
    )(
        statistics.reshape(blocks * 8, 128),
        gradients.reshape(blocks * 4, 128),
        assign.T,
        counts.reshape(1, -1),
    )
    inverse_roots = roots.reshape(statistics.shape)
    root_diagonals = jnp.transpose(diags, (2, 0, 1))
    return inverse_roots, root_diagonals, dirs[None]


def solution(mesh):
    return jax.shard_map(
        per_device,
        mesh=mesh,
        in_specs=(P(None, None, "wide", "narrow"), P(None, "wide", "narrow"), P(), P()),
        out_specs=(
            P(None, None, "wide", "narrow"),
            P(None, None, "wide"),
            P("wide", None, None, None),
        ),
        check_vma=False,
    )
```

```python
import jax
import jax.numpy as jnp
from jax import lax
from jax.experimental import pallas as pl
from jax.experimental.pallas import tpu as pltpu
from jax.sharding import PartitionSpec as P

BLOCK = 512
CHIPS = 64
MESH = pl.DeviceIdType.MESH
F32 = jnp.float32
BF16 = jnp.bfloat16


def far_first():
    sizes = [(a, b) for a in range(5) for b in range(5)]
    sizes.sort(key=lambda s: (-(s[0] + s[1]), abs(s[0] - s[1])))
    order = []
    for a, b in sizes:
        for step in ((a, b), (-a, -b), (a, -b), (-a, b)):
            step = (step[0] % 8, step[1] % 8)
            if step not in order:
                order.append(step)
    return order


STEPS = far_first()
OWN = CHIPS - 1
HALVES = (range(32), range(32, OWN))


def dot(first, second):
    return jnp.dot(first, second, preferred_element_type=F32)


def dot_nt(first, second):
    return lax.dot_general(
        first, second, (((1,), (1,)), ((), ())), preferred_element_type=F32
    )


def iota(shape, axis):
    return lax.broadcasted_iota(jnp.int32, shape, axis)


def hot(condition):
    return jnp.where(condition, 1.0, 0.0).astype(BF16)


def send(src, dst, send_sem, recv_sem, wide, narrow):
    pltpu.make_async_remote_copy(
        src_ref=src,
        dst_ref=dst,
        send_sem=send_sem,
        recv_sem=recv_sem,
        device_id=(wide, narrow),
        device_id_type=MESH,
    ).start()


def wait(ref, sem):
    pltpu.make_async_copy(ref, ref, sem).wait()


def kernel(
    stat_hbm,
    grad_hbm,
    assign_hbm,
    counts_hbm,
    roots_ref,
    diag_ref,
    dirs_ref,
    stat_ref,
    grad_ref,
    assign_ref,
    counts_ref,
    out1,
    in1,
    flat1,
    out2,
    in2,
    gflat,
    gspread,
    gout1,
    gin1,
    gmid,
    gout2,
    gin2,
    grows,
    grad,
    factor,
    work,
    low_a,
    low_b,
    low_root,
    half_out,
    half_in,
    dir_out,
    spread3,
    out3,
    in3,
    flat3,
    out4,
    in4,
    flat4,
    partial,
    diag_pick,
    diag_out,
    diag_in,
    diag_out2,
    diag_in2,
    load_sem,
    send1,
    recv1,
    send2,
    recv2,
    gsend1,
    grecv1,
    gsend2,
    grecv2,
    prod_send,
    prod_recv,
    dir_send,
    dir_recv,
    send3,
    recv3,
    send4,
    recv4,
    diag_send,
    diag_recv,
    diag_send2,
    diag_recv2,
):
    loads = [
        pltpu.make_async_copy(src, dst, load_sem.at[i])
        for i, (src, dst) in enumerate(
            [
                (assign_hbm, assign_ref),
                (counts_hbm, counts_ref),
                (stat_hbm, stat_ref),
                (grad_hbm, grad_ref),
            ]
        )
    ]
    for load in loads:
        load.start()
    wide = lax.axis_index("wide")
    me_n = lax.axis_index("narrow")
    me_j = wide // 2
    me_c = wide % 2
    me_y = me_j % 8
    me_z = me_j // 8
    me_g = me_n * 2 + me_c
    along_y = [(me_y + s) % 8 for s in range(8)]
    along_z = [(me_z + s) % 8 * 8 for s in range(8)]

    def chip(place):
        y, z = STEPS[place]
        return along_z[z] + along_y[y]

    def group_mate(i):
        g = (me_g + i) % 8
        return g, me_j * 2 + g % 2, g // 2

    barrier = pltpu.get_barrier_semaphore()
    for i in range(1, 8):
        _, w, n = group_mate(i)
        pl.semaphore_signal(barrier, inc=1, device_id=(w, n), device_id_type=MESH)
    for place in range(OWN):
        pl.semaphore_signal(
            barrier, inc=1, device_id=(chip(place) * 2 + me_c, me_n), device_id_type=MESH
        )

    def steps_column(which):
        tiles = []
        for start in range(0, CHIPS, 8):
            tile = jnp.full((8, 128), STEPS[start][which], jnp.int32)
            for i in range(1, 8):
                tile = jnp.where(iota((8, 128), 0) == i, STEPS[start + i][which], tile)
            tiles.append(tile)
        return jnp.concatenate(tiles, axis=0)

    step_y, step_z = steps_column(0), steps_column(1)
    to_worker = 2 * ((me_z + step_z) % 8 * 8 + (me_y + step_y) % 8)
    from_worker = 2 * ((me_z - step_z + 8) % 8 * 8 + (me_y - step_y + 8) % 8)
    worker = iota((CHIPS, 128), 1)
    for n in range(4):
        columns = iota((CHIPS, 128), 1) + 128 * n
        diag_pick[:, 128 * n : 128 * n + 128] = hot(columns // 8 * 2 == to_worker)
    loads[0].wait()
    loads[1].wait()
    listed = []
    taken = []
    for slot in range(2):
        match = iota((128, 128), 0) == assign_ref[slot : slot + 1, :]
        listed.append(hot(match))
        taken.append(hot(jnp.logical_and(match, counts_ref[...] > slot)))
    gathers = []
    selects = []
    for m in range(4):
        par, slot = m // 2, m % 2
        gathers.append(dot_nt(hot(worker == to_worker + par), listed[slot]).astype(BF16))
        selects.append(dot_nt(taken[slot], hot(worker == from_worker + par)).astype(BF16))
    gather = jnp.concatenate(gathers, axis=0)

    loads[2].wait()
    for k in range(2):
        for r in range(4):
            x = stat_ref[pl.ds(k * 4 + r, 128, stride=8), :]
            high = x.astype(BF16).astype(F32)
            upper = iota((128, 128), 1) + 128 * me_n >= 4 * wide + r
            mixed = jnp.where(upper, high, x - high).astype(BF16)
            picked = dot(gather, mixed).astype(BF16)
            for m in range(4):
                for half in range(2):
                    start = m * 64 + half * 32
                    out1[half, m * 2 + k, r * 32 : r * 32 + 32, :] = picked[start : start + 32]
    for half in range(2):
        in1[half, me_g] = out1[half, me_g]
    loads[3].wait()
    gflat[...] = grad_ref[...].astype(F32)
    for r in range(4):
        x = gflat[pl.ds(r, 128, stride=4), :].astype(BF16)
        picked = dot(gather, x)
        for m in range(4):
            gspread[pl.ds(m * 4 + r, 64, stride=16), :] = picked[m * 64 : m * 64 + 64]
    gout1[...] = gspread[...].reshape(CHIPS, 16, 128).astype(BF16)
    gin1[me_j] = gout1[OWN]

    pl.semaphore_wait(barrier, 70)

    for half in range(2):
        for i in (4, 5, 3, 2, 6, 7, 1):
            g, w, n = group_mate(i)
            send(
                out1.at[half, g], in1.at[half, me_g], send1.at[half], recv1.at[half], w, n
            )
    for place in range(OWN):
        send(
            gout1.at[place], gin1.at[me_j], gsend1, grecv1, chip(place) * 2 + me_c, me_n
        )

    for half, places in enumerate(HALVES):
        wait(in1.at[half, pl.ds(0, 7)], recv1.at[half])
        flat1[half] = in1[half].reshape(1024, 128).astype(F32)
        if half == 1:
            out2[OWN] = flat1[1, pl.ds(OWN - 32, 32, stride=32), :].astype(BF16)
            in2[me_j] = out2[OWN]
        for place in places:
            out2[place] = flat1[half, pl.ds(place % 32, 32, stride=32), :].astype(BF16)
            send(
                out2.at[place], in2.at[me_j], send2, recv2, chip(place) * 2 + me_c, me_n
            )

    wait(gin1.at[pl.ds(0, CHIPS - 1)], grecv1)
    gmid[...] = gin1[...].reshape(1024, 128).astype(F32)
    for m in range(4):
        for r in range(4):
            gout2[m, r * 64 : r * 64 + 64, :] = gmid[pl.ds(m * 4 + r, 64, stride=16), :].astype(
                BF16
            )
    for d in (2, 1, 3):
        m = (me_n + d) % 4
        send(gout2.at[m], gin2.at[me_g], gsend2, grecv2, me_j * 2, m)

    @pl.when(me_c == 1)
    def _():
        send(gout2.at[me_n], gin2.at[me_g], gsend2, grecv2, me_j * 2, me_n)

    @pl.when(me_c == 0)
    def _():
        gin2[me_g] = gout2[me_n]

    wait(in2.at[pl.ds(0, CHIPS - 1)], recv2)
    for j in range(CHIPS):
        x = in2[j].astype(F32)
        for n in range(4):
            factor[8 * j : 8 * j + 8, 128 * n : 128 * n + 128] = x[8 * n : 8 * n + 8]

    eye = iota((BLOCK, BLOCK), 0) == iota((BLOCK, BLOCK), 1)
    received = factor[...]
    a = received + jnp.where(eye, 0.0, received.T)
    total = jnp.sum(jnp.sum(a * a, axis=0, keepdims=True), axis=1, keepdims=True)
    scaling = 2.5 / jnp.sqrt(total)
    c = scaling * a
    factor[...] = c
    low_a[...] = c.astype(BF16)
    e = dot(low_a[...], low_a[...]) - 10.0 * factor[...]
    work[...] = e
    low_b[...] = e.astype(BF16)
    f = 50.0 * work[...] + dot(low_b[...], low_b[...])
    low_b[...] = f.astype(BF16)
    c2 = (625.0 / 256.0) * factor[...] + (1.0 / 256.0) * dot(low_b[...], low_a[...])
    work[...] = c2
    low_b[...] = c2.astype(BF16)
    scale4 = jnp.sqrt(jnp.sqrt(scaling)) * (1.0 / 16.0)
    tail = dot(low_a[...], low_b[...]) - 5.0 * (factor[...] + work[...])
    root = scale4 * (jnp.where(eye, 25.0, 0.0) + tail)
    work[...] = root
    low_root[...] = root.astype(BF16)
    diagonal = jnp.sum(jnp.where(eye, root, 0.0), axis=0, keepdims=True)
    spread = jnp.where(iota((16, BLOCK), 1) % 8 == iota((16, BLOCK), 0), diagonal, 0.0)
    diag_out[...] = jnp.concatenate(
        [dot_nt(spread.astype(BF16), diag_pick[...]), jnp.zeros((16, CHIPS), F32)], axis=1
    ).astype(BF16)
    diag_in[me_g] = diag_out[...]

    for i in (4, 5, 3, 2, 6, 7, 1):
        g, w, n = group_mate(i)
        send(diag_out, diag_in.at[me_g], diag_send, diag_recv, w, n)
    for half, places in enumerate((range(32), range(32, CHIPS))):
        for i, place in enumerate(places):
            rows = pl.ds(pl.multiple_of(chip(place) * 8, 8), 8)
            for n in range(4):
                spread3[n, i * 8 : i * 8 + 8, :] = work[rows, 128 * n : 128 * n + 128]
        for q in range(32):
            n, core, r = q // 8, q // 4 % 2, q % 4
            out3[half, n * 2 + core, r * 32 : r * 32 + 32, :] = spread3[
                n, pl.ds(core * 4 + r, 32, stride=8), :
            ].astype(BF16)
        in3[half, me_g] = out3[half, me_g]
        for i in (4, 5, 3, 2, 6, 7, 1):
            g, w, n = group_mate(i)
            send(
                out3.at[half, g], in3.at[half, me_g], send3.at[half], recv3.at[half], w, n
            )

    @pl.when(me_c == 0)
    def _():
        wait(gin2.at[pl.ds(0, 7)], grecv2)
        for g in range(8):
            for r in range(4):
                grows[g // 2, pl.ds(g % 2 * 4 + r, 64, stride=8), :] = gin2[
                    g, r * 64 : r * 64 + 64, :
                ].astype(F32)
        for n in range(4):
            grad[:, 128 * n : 128 * n + 128] = grows[n].astype(BF16)
        half_out[...] = dot(low_root[...], grad[...]).astype(BF16)
        send(half_out, half_in, prod_send, prod_recv, me_j * 2 + 1, me_n)

    def send_diagonals():
        wait(diag_in.at[pl.ds(0, 7)], diag_recv)
        tiles = []
        for g in range(8):
            tile = diag_in[g].astype(F32)
            tiles.append(jnp.where(me_c == 0, tile[0:4], tile[4:8]))
        tiles.append(jnp.zeros((96, 128), F32))
        diag_out2[...] = jnp.concatenate(tiles, axis=0).T[:CHIPS].reshape(CHIPS, 1, 128)
        for place in range(OWN):
            send(
                diag_out2.at[place],
                diag_in2.at[place],
                diag_send2,
                diag_recv2,
                chip(place) * 2 + me_c,
                me_n,
            )
        diag_in2[OWN] = diag_out2[OWN]

    def send_directions():
        @pl.when(me_c == 1)
        def _():
            mine = jnp.logical_and(
                iota((1, 128), 1) == 2 * me_j + me_n // 2, counts_ref[...] > me_n % 2
            )
            keep = jnp.sum(jnp.where(mine, 1.0, 0.0), axis=1, keepdims=True)
            wait(half_in, prod_recv)
            dir_out[...] = (dot(half_in[...], low_root[...]) * keep).astype(BF16)
            for d in (2, 1, 3):
                send(
                    dir_out,
                    dirs_ref.at[me_n % 2],
                    dir_send,
                    dir_recv.at[me_n % 2],
                    me_j * 2 + me_n // 2,
                    (me_n + d) % 4,
                )

        @pl.when(jnp.logical_and(me_c == 1, me_n // 2 == 0))
        def _():
            send(
                dir_out,
                dirs_ref.at[me_n % 2],
                dir_send,
                dir_recv.at[me_n % 2],
                me_j * 2,
                me_n,
            )

        @pl.when(jnp.logical_and(me_c == 1, me_n // 2 == 1))
        def _():
            dirs_ref[me_n % 2] = dir_out[...]

    for half, places in enumerate(HALVES):
        if half == 1:
            send_diagonals()
            send_directions()
        wait(in3.at[half, pl.ds(0, 7)], recv3.at[half])
        flat3[half] = in3[half].reshape(1024, 128).astype(F32)
        for place in places:
            out4[place] = flat3[half, pl.ds(place % 32, 32, stride=32), :].astype(BF16)
            send(
                out4.at[place],
                in4.at[place],
                send4,
                recv4.at[half],
                chip(place) * 2 + me_c,
                me_n,
            )
        if half == 1:
            in4[OWN] = flat3[half, pl.ds(OWN % 32, 32, stride=32), :].astype(BF16)

    def picked_rows(k, r, half):
        select = jnp.concatenate([s[:, half * 32 : half * 32 + 32] for s in selects], axis=1)
        starts = [half * 1024 + (m * 2 + k) * 4 + r for m in range(4)]
        rows = [flat4[pl.ds(start, 32, stride=32), :].astype(BF16) for start in starts]
        return dot(select, jnp.concatenate(rows, axis=0))

    wait(in4.at[pl.ds(0, 32)], recv4.at[0])
    flat4[:1024] = in4[:32].reshape(1024, 128).astype(F32)
    for k in range(2):
        for r in range(4):
            partial[k * 4 + r] = picked_rows(k, r, 0)
    wait(diag_in2.at[pl.ds(0, OWN)], diag_recv2)
    by_slot = diag_in2[...].reshape(CHIPS, 128).T[:32].astype(BF16)
    diag = jnp.zeros((8, 128), F32)
    for m in range(4):
        diag = diag + dot_nt(by_slot, selects[m])[8 * m : 8 * m + 8]
    for k in range(2):
        diag_ref[k] = diag[4 * k : 4 * k + 4]
    wait(in4.at[pl.ds(0, 31)], recv4.at[1])
    flat4[1024:] = in4[32:].reshape(1024, 128).astype(F32)
    for k in range(2):
        for r in range(4):
            full = partial[k * 4 + r] + picked_rows(k, r, 1)
            on_diag = iota((128, 128), 1) + 128 * me_n == 4 * wide + r
            roots_ref[pl.ds(k * 4 + r, 128, stride=8), :] = jnp.where(on_diag, 0.0, full)

    @pl.when(jnp.logical_and(me_c == 1, me_n == 2))
    def _():
        wait(dirs_ref.at[1], dir_recv.at[1])

    @pl.when(jnp.logical_and(me_c == 1, me_n == 3))
    def _():
        wait(dirs_ref.at[0], dir_recv.at[0])

    @pl.when(jnp.logical_or(me_c == 0, me_n < 2))
    def _():
        wait(dirs_ref.at[0], dir_recv.at[0])
        wait(dirs_ref.at[1], dir_recv.at[1])

    for half in range(2):
        wait(in1.at[half, pl.ds(0, 7)], send1.at[half])
    wait(in2.at[pl.ds(0, CHIPS - 1)], send2)
    wait(gin1.at[pl.ds(0, CHIPS - 1)], gsend1)
    for half in range(2):
        wait(in3.at[half, pl.ds(0, 7)], send3.at[half])
    wait(in4.at[pl.ds(0, CHIPS - 1)], send4)
    wait(diag_in.at[pl.ds(0, 7)], diag_send)
    wait(diag_in2.at[pl.ds(0, OWN)], diag_send2)

    @pl.when(me_c == 0)
    def _():
        wait(gin2.at[pl.ds(0, 3)], gsend2)
        wait(half_in, prod_send)

    @pl.when(me_c == 1)
    def _():
        wait(gin2.at[pl.ds(0, 4)], gsend2)

    @pl.when(jnp.logical_and(me_c == 1, me_n // 2 == 0))
    def _():
        wait(dirs_ref, dir_send)
        wait(dirs_ref, dir_send)

    @pl.when(jnp.logical_and(me_c == 1, me_n // 2 == 1))
    def _():
        wait(dirs_ref, dir_send)
        wait(dirs_ref.at[0], dir_send)


def per_device(statistics, gradients, assign, counts):
    blocks = statistics.shape[0]
    vmem = pl.BlockSpec(memory_space=pltpu.VMEM)
    hbm = pl.BlockSpec(memory_space=pltpu.HBM)
    square = (BLOCK, BLOCK)
    shapes = [
        ((blocks * 8, 128), F32),
        ((blocks * 4, 128), BF16),
        ((2, 128), jnp.int32),
        ((1, 128), jnp.int32),
        ((2, 8, 128, 128), BF16),
        ((2, 8, 128, 128), BF16),
        ((2, 1024, 128), F32),
        ((64, 32, 128), BF16),
        ((64, 32, 128), BF16),
        ((512, 128), F32),
        ((1024, 128), F32),
        ((64, 16, 128), BF16),
        ((64, 16, 128), BF16),
        ((1024, 128), F32),
        ((4, 256, 128), BF16),
        ((8, 256, 128), BF16),
        ((4, 512, 128), F32),
        (square, BF16),
        (square, F32),
        (square, F32),
        (square, BF16),
        (square, BF16),
        (square, BF16),
        (square, BF16),
        (square, BF16),
        (square, BF16),
        ((4, 256, 128), F32),
        ((2, 8, 128, 128), BF16),
        ((2, 8, 128, 128), BF16),
        ((2, 1024, 128), F32),
        ((64, 32, 128), BF16),
        ((64, 32, 128), BF16),
        ((2048, 128), F32),
        ((8, 128, 128), F32),
        ((64, BLOCK), BF16),
        ((16, 128), BF16),
        ((8, 16, 128), BF16),
        ((64, 1, 128), F32),
        ((64, 1, 128), F32),
    ]
    dma = pltpu.SemaphoreType.DMA
    two = dma((2,))
    scratch = [pltpu.VMEM(shape, dtype) for shape, dtype in shapes]
    scratch += [dma((4,)), two, two] + [dma] * 9 + [two] * 3 + [dma, two] + [dma] * 4
    roots, diags, dirs = pl.pallas_call(
        kernel,
        out_shape=[
            jax.ShapeDtypeStruct((blocks * 8, 128), F32),
            jax.ShapeDtypeStruct((2, 4, blocks), F32),
            jax.ShapeDtypeStruct((2, BLOCK, BLOCK), BF16),
        ],
        in_specs=[hbm] * 4,
        out_specs=[vmem, vmem, vmem],
        scratch_shapes=scratch,
        compiler_params=pltpu.CompilerParams(
            collective_id=0, has_side_effects=True, vmem_limit_bytes=40 * 2**20
        ),
        cost_estimate=pl.CostEstimate(
            flops=2 * 6 * BLOCK**3, bytes_accessed=4 * 2**20, transcendentals=0
        ),
        name="shampoo_roots",
    )(
        *(
            pltpu.with_memory_space_constraint(x, pltpu.HBM)
            for x in (
                statistics.reshape(blocks * 8, 128),
                gradients.reshape(blocks * 4, 128),
                assign.T,
                counts.reshape(1, -1),
            )
        ),
    )
    inverse_roots = roots.reshape(statistics.shape)
    root_diagonals = jnp.transpose(diags, (2, 0, 1))
    return inverse_roots, root_diagonals, dirs[None]


def solution(mesh):
    return jax.shard_map(
        per_device,
        mesh=mesh,
        in_specs=(P(None, None, "wide", "narrow"), P(None, "wide", "narrow"), P(), P()),
        out_specs=(
            P(None, None, "wide", "narrow"),
            P(None, None, "wide"),
            P("wide", None, None, None),
        ),
        check_vma=False,
    )
```

```python
import jax
import jax.numpy as jnp
from jax import lax
from jax.experimental import pallas as pl
from jax.experimental.pallas import tpu as pltpu
from jax.sharding import PartitionSpec as P

BLOCK = 512
CHIPS = 64
MESH = pl.DeviceIdType.MESH
F32 = jnp.float32
BF16 = jnp.bfloat16


def far_first():
    sizes = [(a, b) for a in range(5) for b in range(5)]
    sizes.sort(key=lambda s: (-max(s), -(s[0] + s[1])))
    order = []
    for a, b in sizes:
        for step in ((a, b), (-a, -b), (a, -b), (-a, b)):
            step = (step[0] % 8, step[1] % 8)
            if step not in order:
                order.append(step)
    return order


STEPS = far_first()
OWN = CHIPS - 1
HALVES = (range(32), range(32, OWN))


def dot(first, second):
    return jnp.dot(first, second, preferred_element_type=F32)


def dot_nt(first, second):
    return lax.dot_general(
        first, second, (((1,), (1,)), ((), ())), preferred_element_type=F32
    )


def iota(shape, axis):
    return lax.broadcasted_iota(jnp.int32, shape, axis)


def hot(condition):
    return jnp.where(condition, 1.0, 0.0).astype(BF16)


def send(src, dst, send_sem, recv_sem, wide, narrow):
    pltpu.make_async_remote_copy(
        src_ref=src,
        dst_ref=dst,
        send_sem=send_sem,
        recv_sem=recv_sem,
        device_id=(wide, narrow),
        device_id_type=MESH,
    ).start()


def wait(ref, sem):
    pltpu.make_async_copy(ref, ref, sem).wait()


def kernel(
    stat_hbm,
    grad_hbm,
    assign_hbm,
    counts_hbm,
    roots_ref,
    diag_ref,
    dirs_ref,
    stat_ref,
    grad_ref,
    assign_ref,
    counts_ref,
    out1,
    in1,
    flat1,
    out2,
    in2,
    gflat,
    gspread,
    gout1,
    gin1,
    gmid,
    gout2,
    gin2,
    grows,
    grad,
    factor,
    work,
    low_a,
    low_b,
    low_root,
    half_out,
    half_in,
    dir_out,
    spread3,
    out3,
    in3,
    flat3,
    out4,
    in4,
    flat4,
    partial,
    diag_pick,
    diag_out,
    diag_in,
    diag_out2,
    diag_in2,
    load_sem,
    send1,
    recv1,
    send2,
    recv2,
    gsend1,
    grecv1,
    gsend2,
    grecv2,
    prod_send,
    prod_recv,
    dir_send,
    dir_recv,
    send3,
    recv3,
    send4,
    recv4,
    diag_send,
    diag_recv,
    diag_send2,
    diag_recv2,
):
    loads = [
        pltpu.make_async_copy(src, dst, load_sem.at[i])
        for i, (src, dst) in enumerate(
            [
                (assign_hbm, assign_ref),
                (counts_hbm, counts_ref),
                (stat_hbm, stat_ref),
                (grad_hbm, grad_ref),
            ]
        )
    ]
    for load in loads:
        load.start()
    wide = lax.axis_index("wide")
    me_n = lax.axis_index("narrow")
    me_j = wide // 2
    me_c = wide % 2
    me_y = me_j % 8
    me_z = me_j // 8
    me_g = me_n * 2 + me_c
    along_y = [(me_y + s) % 8 for s in range(8)]
    along_z = [(me_z + s) % 8 * 8 for s in range(8)]

    def chip(place):
        y, z = STEPS[place]
        return along_z[z] + along_y[y]

    def group_mate(i):
        g = (me_g + i) % 8
        return g, me_j * 2 + g % 2, g // 2

    barrier = pltpu.get_barrier_semaphore()
    for i in range(1, 8):
        _, w, n = group_mate(i)
        pl.semaphore_signal(barrier, inc=1, device_id=(w, n), device_id_type=MESH)
    for place in range(OWN):
        pl.semaphore_signal(
            barrier, inc=1, device_id=(chip(place) * 2 + me_c, me_n), device_id_type=MESH
        )

    def steps_column(which):
        tiles = []
        for start in range(0, CHIPS, 8):
            tile = jnp.full((8, 128), STEPS[start][which], jnp.int32)
            for i in range(1, 8):
                tile = jnp.where(iota((8, 128), 0) == i, STEPS[start + i][which], tile)
            tiles.append(tile)
        return jnp.concatenate(tiles, axis=0)

    step_y, step_z = steps_column(0), steps_column(1)
    to_worker = 2 * ((me_z + step_z) % 8 * 8 + (me_y + step_y) % 8)
    from_worker = 2 * ((me_z - step_z + 8) % 8 * 8 + (me_y - step_y + 8) % 8)
    worker = iota((CHIPS, 128), 1)
    for n in range(4):
        columns = iota((CHIPS, 128), 1) + 128 * n
        diag_pick[:, 128 * n : 128 * n + 128] = hot(columns // 8 * 2 == to_worker)
    loads[0].wait()
    loads[1].wait()
    listed = []
    taken = []
    for slot in range(2):
        match = iota((128, 128), 0) == assign_ref[slot : slot + 1, :]
        listed.append(hot(match))
        taken.append(hot(jnp.logical_and(match, counts_ref[...] > slot)))
    gathers = []
    selects = []
    for m in range(4):
        par, slot = m // 2, m % 2
        gathers.append(dot_nt(hot(worker == to_worker + par), listed[slot]).astype(BF16))
        selects.append(dot_nt(taken[slot], hot(worker == from_worker + par)).astype(BF16))
    gather = jnp.concatenate(gathers, axis=0)

    loads[2].wait()
    for k in range(2):
        for r in range(4):
            x = stat_ref[pl.ds(k * 4 + r, 128, stride=8), :]
            high = x.astype(BF16).astype(F32)
            upper = iota((128, 128), 1) + 128 * me_n >= 4 * wide + r
            mixed = jnp.where(upper, high, x - high).astype(BF16)
            picked = dot(gather, mixed).astype(BF16)
            for m in range(4):
                for half in range(2):
                    start = m * 64 + half * 32
                    out1[half, m * 2 + k, r * 32 : r * 32 + 32, :] = picked[start : start + 32]
    for half in range(2):
        in1[half, me_g] = out1[half, me_g]

    pl.semaphore_wait(barrier, 70)

    for half in range(2):
        for i in (4, 5, 3, 2, 6, 7, 1):
            g, w, n = group_mate(i)
            send(
                out1.at[half, g], in1.at[half, me_g], send1.at[half], recv1.at[half], w, n
            )
    loads[3].wait()
    gflat[...] = grad_ref[...].astype(F32)
    for r in range(4):
        x = gflat[pl.ds(r, 128, stride=4), :].astype(BF16)
        picked = dot(gather, x)
        for m in range(4):
            gspread[pl.ds(m * 4 + r, 64, stride=16), :] = picked[m * 64 : m * 64 + 64]
    gout1[...] = gspread[...].reshape(CHIPS, 16, 128).astype(BF16)
    gin1[me_j] = gout1[OWN]
    for place in range(OWN):
        send(
            gout1.at[place], gin1.at[me_j], gsend1, grecv1, chip(place) * 2 + me_c, me_n
        )

    for half, places in enumerate(HALVES):
        wait(in1.at[half, pl.ds(0, 7)], recv1.at[half])
        flat1[half] = in1[half].reshape(1024, 128).astype(F32)
        if half == 1:
            out2[OWN] = flat1[1, pl.ds(OWN - 32, 32, stride=32), :].astype(BF16)
            in2[me_j] = out2[OWN]
        for place in places:
            out2[place] = flat1[half, pl.ds(place % 32, 32, stride=32), :].astype(BF16)
            send(
                out2.at[place], in2.at[me_j], send2, recv2, chip(place) * 2 + me_c, me_n
            )

    wait(gin1.at[pl.ds(0, CHIPS - 1)], grecv1)
    gmid[...] = gin1[...].reshape(1024, 128).astype(F32)
    for m in range(4):
        for r in range(4):
            gout2[m, r * 64 : r * 64 + 64, :] = gmid[pl.ds(m * 4 + r, 64, stride=16), :].astype(
                BF16
            )
    for d in (2, 1, 3):
        m = (me_n + d) % 4
        send(gout2.at[m], gin2.at[me_g], gsend2, grecv2, me_j * 2, m)

    @pl.when(me_c == 1)
    def _():
        send(gout2.at[me_n], gin2.at[me_g], gsend2, grecv2, me_j * 2, me_n)

    @pl.when(me_c == 0)
    def _():
        gin2[me_g] = gout2[me_n]

    wait(in2.at[pl.ds(0, CHIPS - 1)], recv2)
    for j in range(CHIPS):
        x = in2[j].astype(F32)
        for n in range(4):
            factor[8 * j : 8 * j + 8, 128 * n : 128 * n + 128] = x[8 * n : 8 * n + 8]

    eye = iota((BLOCK, BLOCK), 0) == iota((BLOCK, BLOCK), 1)
    received = factor[...]
    a = received + jnp.where(eye, 0.0, received.T)
    total = jnp.sum(jnp.sum(a * a, axis=0, keepdims=True), axis=1, keepdims=True)
    scaling = 2.5 / jnp.sqrt(total)
    c = scaling * a
    factor[...] = c
    low_a[...] = c.astype(BF16)
    e = dot(low_a[...], low_a[...]) - 10.0 * factor[...]
    work[...] = e
    low_b[...] = e.astype(BF16)
    f = 50.0 * work[...] + dot(low_b[...], low_b[...])
    low_b[...] = f.astype(BF16)
    c2 = (625.0 / 256.0) * factor[...] + (1.0 / 256.0) * dot(low_b[...], low_a[...])
    work[...] = c2
    low_b[...] = c2.astype(BF16)
    scale4 = jnp.sqrt(jnp.sqrt(scaling)) * (1.0 / 16.0)
    tail = dot(low_a[...], low_b[...]) - 5.0 * (factor[...] + work[...])
    root = scale4 * (jnp.where(eye, 25.0, 0.0) + tail)
    work[...] = root
    low_root[...] = root.astype(BF16)

    for half, places in enumerate((range(32), range(32, CHIPS))):
        for i, place in enumerate(places):
            rows = pl.ds(pl.multiple_of(chip(place) * 8, 8), 8)
            for n in range(4):
                spread3[n, i * 8 : i * 8 + 8, :] = work[rows, 128 * n : 128 * n + 128]
        for q in range(32):
            n, core, r = q // 8, q // 4 % 2, q % 4
            out3[half, n * 2 + core, r * 32 : r * 32 + 32, :] = spread3[
                n, pl.ds(core * 4 + r, 32, stride=8), :
            ].astype(BF16)
        in3[half, me_g] = out3[half, me_g]
        for i in (4, 5, 3, 2, 6, 7, 1):
            g, w, n = group_mate(i)
            send(
                out3.at[half, g], in3.at[half, me_g], send3.at[half], recv3.at[half], w, n
            )

    diagonal = jnp.sum(jnp.where(eye, work[...], 0.0), axis=0, keepdims=True)
    spread = jnp.where(iota((16, BLOCK), 1) % 8 == iota((16, BLOCK), 0), diagonal, 0.0)
    diag_out[...] = jnp.concatenate(
        [dot_nt(spread.astype(BF16), diag_pick[...]), jnp.zeros((16, CHIPS), F32)], axis=1
    ).astype(BF16)
    diag_in[me_g] = diag_out[...]
    for i in (4, 5, 3, 2, 6, 7, 1):
        g, w, n = group_mate(i)
        send(diag_out, diag_in.at[me_g], diag_send, diag_recv, w, n)

    @pl.when(me_c == 0)
    def _():
        wait(gin2.at[pl.ds(0, 7)], grecv2)
        for g in range(8):
            for r in range(4):
                grows[g // 2, pl.ds(g % 2 * 4 + r, 64, stride=8), :] = gin2[
                    g, r * 64 : r * 64 + 64, :
                ].astype(F32)
        for n in range(4):
            grad[:, 128 * n : 128 * n + 128] = grows[n].astype(BF16)
        half_out[...] = dot(low_root[...], grad[...]).astype(BF16)
        send(half_out, half_in, prod_send, prod_recv, me_j * 2 + 1, me_n)

    def send_diagonals():
        wait(diag_in.at[pl.ds(0, 7)], diag_recv)
        tiles = []
        for g in range(8):
            tile = diag_in[g].astype(F32)
            tiles.append(jnp.where(me_c == 0, tile[0:4], tile[4:8]))
        tiles.append(jnp.zeros((96, 128), F32))
        diag_out2[...] = jnp.concatenate(tiles, axis=0).T[:CHIPS].reshape(CHIPS, 1, 128)
        for place in range(OWN):
            send(
                diag_out2.at[place],
                diag_in2.at[place],
                diag_send2,
                diag_recv2,
                chip(place) * 2 + me_c,
                me_n,
            )
        diag_in2[OWN] = diag_out2[OWN]

    def send_directions():
        @pl.when(me_c == 1)
        def _():
            mine = jnp.logical_and(
                iota((1, 128), 1) == 2 * me_j + me_n // 2, counts_ref[...] > me_n % 2
            )
            keep = jnp.sum(jnp.where(mine, 1.0, 0.0), axis=1, keepdims=True)
            wait(half_in, prod_recv)
            dir_out[...] = (dot(half_in[...], low_root[...]) * keep).astype(BF16)
            for d in (2, 1, 3):
                send(
                    dir_out,
                    dirs_ref.at[me_n % 2],
                    dir_send,
                    dir_recv.at[me_n % 2],
                    me_j * 2 + me_n // 2,
                    (me_n + d) % 4,
                )

        @pl.when(jnp.logical_and(me_c == 1, me_n // 2 == 0))
        def _():
            send(
                dir_out,
                dirs_ref.at[me_n % 2],
                dir_send,
                dir_recv.at[me_n % 2],
                me_j * 2,
                me_n,
            )

        @pl.when(jnp.logical_and(me_c == 1, me_n // 2 == 1))
        def _():
            dirs_ref[me_n % 2] = dir_out[...]

    for half, places in enumerate(HALVES):
        if half == 1:
            send_diagonals()
            send_directions()
        wait(in3.at[half, pl.ds(0, 7)], recv3.at[half])
        flat3[half] = in3[half].reshape(1024, 128).astype(F32)
        for place in places:
            out4[place] = flat3[half, pl.ds(place % 32, 32, stride=32), :].astype(BF16)
            send(
                out4.at[place],
                in4.at[place],
                send4,
                recv4.at[half],
                chip(place) * 2 + me_c,
                me_n,
            )
        if half == 1:
            in4[OWN] = flat3[half, pl.ds(OWN % 32, 32, stride=32), :].astype(BF16)

    by_half = [
        jnp.concatenate([s[:, half * 32 : half * 32 + 32] for s in selects], axis=1)
        for half in range(2)
    ]

    def picked_rows(k, r, half):
        starts = [half * 1024 + (m * 2 + k) * 4 + r for m in range(4)]
        rows = [flat4[pl.ds(start, 32, stride=32), :].astype(BF16) for start in starts]
        return dot(by_half[half], jnp.concatenate(rows, axis=0))

    wait(in4.at[pl.ds(0, 32)], recv4.at[0])
    flat4[:1024] = in4[:32].reshape(1024, 128).astype(F32)
    for k in range(2):
        for r in range(4):
            partial[k * 4 + r] = picked_rows(k, r, 0)
    wait(diag_in2.at[pl.ds(0, OWN)], diag_recv2)
    by_slot = diag_in2[...].reshape(CHIPS, 128).T[:32].astype(BF16)
    diag = jnp.zeros((8, 128), F32)
    for m in range(4):
        diag = diag + dot_nt(by_slot, selects[m])[8 * m : 8 * m + 8]
    for k in range(2):
        diag_ref[k] = diag[4 * k : 4 * k + 4]
    wait(in4.at[pl.ds(0, 31)], recv4.at[1])
    flat4[1024:] = in4[32:].reshape(1024, 128).astype(F32)
    for k in range(2):
        for r in range(4):
            full = partial[k * 4 + r] + picked_rows(k, r, 1)
            on_diag = iota((128, 128), 1) + 128 * me_n == 4 * wide + r
            roots_ref[pl.ds(k * 4 + r, 128, stride=8), :] = jnp.where(on_diag, 0.0, full)

    @pl.when(jnp.logical_and(me_c == 1, me_n == 2))
    def _():
        wait(dirs_ref.at[1], dir_recv.at[1])

    @pl.when(jnp.logical_and(me_c == 1, me_n == 3))
    def _():
        wait(dirs_ref.at[0], dir_recv.at[0])

    @pl.when(jnp.logical_or(me_c == 0, me_n < 2))
    def _():
        wait(dirs_ref.at[0], dir_recv.at[0])
        wait(dirs_ref.at[1], dir_recv.at[1])

    for half in range(2):
        wait(in1.at[half, pl.ds(0, 7)], send1.at[half])
    wait(in2.at[pl.ds(0, CHIPS - 1)], send2)
    wait(gin1.at[pl.ds(0, CHIPS - 1)], gsend1)
    for half in range(2):
        wait(in3.at[half, pl.ds(0, 7)], send3.at[half])
    wait(in4.at[pl.ds(0, CHIPS - 1)], send4)
    wait(diag_in.at[pl.ds(0, 7)], diag_send)
    wait(diag_in2.at[pl.ds(0, OWN)], diag_send2)

    @pl.when(me_c == 0)
    def _():
        wait(gin2.at[pl.ds(0, 3)], gsend2)
        wait(half_in, prod_send)

    @pl.when(me_c == 1)
    def _():
        wait(gin2.at[pl.ds(0, 4)], gsend2)

    @pl.when(jnp.logical_and(me_c == 1, me_n // 2 == 0))
    def _():
        wait(dirs_ref, dir_send)
        wait(dirs_ref, dir_send)

    @pl.when(jnp.logical_and(me_c == 1, me_n // 2 == 1))
    def _():
        wait(dirs_ref, dir_send)
        wait(dirs_ref.at[0], dir_send)


def per_device(statistics, gradients, assign, counts):
    blocks = statistics.shape[0]
    vmem = pl.BlockSpec(memory_space=pltpu.VMEM)
    hbm = pl.BlockSpec(memory_space=pltpu.HBM)
    square = (BLOCK, BLOCK)
    shapes = [
        ((blocks * 8, 128), F32),
        ((blocks * 4, 128), BF16),
        ((2, 128), jnp.int32),
        ((1, 128), jnp.int32),
        ((2, 8, 128, 128), BF16),
        ((2, 8, 128, 128), BF16),
        ((2, 1024, 128), F32),
        ((64, 32, 128), BF16),
        ((64, 32, 128), BF16),
        ((512, 128), F32),
        ((1024, 128), F32),
        ((64, 16, 128), BF16),
        ((64, 16, 128), BF16),
        ((1024, 128), F32),
        ((4, 256, 128), BF16),
        ((8, 256, 128), BF16),
        ((4, 512, 128), F32),
        (square, BF16),
        (square, F32),
        (square, F32),
        (square, BF16),
        (square, BF16),
        (square, BF16),
        (square, BF16),
        (square, BF16),
        (square, BF16),
        ((4, 256, 128), F32),
        ((2, 8, 128, 128), BF16),
        ((2, 8, 128, 128), BF16),
        ((2, 1024, 128), F32),
        ((64, 32, 128), BF16),
        ((64, 32, 128), BF16),
        ((2048, 128), F32),
        ((8, 128, 128), F32),
        ((64, BLOCK), BF16),
        ((16, 128), BF16),
        ((8, 16, 128), BF16),
        ((64, 1, 128), F32),
        ((64, 1, 128), F32),
    ]
    dma = pltpu.SemaphoreType.DMA
    two = dma((2,))
    scratch = [pltpu.VMEM(shape, dtype) for shape, dtype in shapes]
    scratch += [dma((4,)), two, two] + [dma] * 9 + [two] * 3 + [dma, two] + [dma] * 4
    roots, diags, dirs = pl.pallas_call(
        kernel,
        out_shape=[
            jax.ShapeDtypeStruct((blocks * 8, 128), F32),
            jax.ShapeDtypeStruct((2, 4, blocks), F32),
            jax.ShapeDtypeStruct((2, BLOCK, BLOCK), BF16),
        ],
        in_specs=[hbm] * 4,
        out_specs=[vmem, vmem, vmem],
        scratch_shapes=scratch,
        compiler_params=pltpu.CompilerParams(
            collective_id=0, has_side_effects=True, vmem_limit_bytes=40 * 2**20
        ),
        cost_estimate=pl.CostEstimate(
            flops=2 * 6 * BLOCK**3, bytes_accessed=4 * 2**20, transcendentals=0
        ),
        name="shampoo_roots",
    )(
        *(
            pltpu.with_memory_space_constraint(x, pltpu.HBM)
            for x in (
                statistics.reshape(blocks * 8, 128),
                gradients.reshape(blocks * 4, 128),
                assign.T,
                counts.reshape(1, -1),
            )
        ),
    )
    inverse_roots = roots.reshape(statistics.shape)
    root_diagonals = jnp.transpose(diags, (2, 0, 1))
    return inverse_roots, root_diagonals, dirs[None]


def solution(mesh):
    return jax.shard_map(
        per_device,
        mesh=mesh,
        in_specs=(P(None, None, "wide", "narrow"), P(None, "wide", "narrow"), P(), P()),
        out_specs=(
            P(None, None, "wide", "narrow"),
            P(None, None, "wide"),
            P("wide", None, None, None),
        ),
        check_vma=False,
    )
```
